32 devices in a mesh: row: 4 (over y, x), col: 8 (over z, core).
Axes of the slice: x: 2, y: 2, z: 4, core: 2. Of those that a mesh axis runs over, the one named last changes fastest.
Arguments:
- atom_blocks: float32 [64, 16, 128, 128], P('row', 'col'), may hold values from -6 to 6
- grid_position: int32 [64], replicated, may hold values from 0 to 63, as said below
- pattern: int32 [64, 16], replicated, may hold values from -1 to 63, as said below
Outputs:
- square: float32 [64, 16, 128, 128], P('row', 'col')
- update: float32 [64, 16, 128, 128], P('row', 'col')
The draws below stay inside these ranges and needn't reach their ends.
Inputs may be any that keep to these rules, and one draw needn't show every extreme that they name: grid_position is a permutation; the 16 atom block rows a with a // 16 equal put at most 4 grid positions into any one run of 16 grid positions that starts at a multiple of 16, and exactly 4 into some run. `pattern`: each row holds 12 different block columns, one of them its own index, and -1 in its other slots; all slots s that hold one block column j have the same s // 2; the block rows lie on a cycle of 64 places, not given, on which each row's columns lie within 16 places in a row around its own.
All inputs are finite; a program needn't handle non-finite values.
Results may differ from the reference program's by a relative error of at most 0.0003.
Values sent between devices are 32-bit elements; how exact they have to be, the bound alone decides.
A program may use at most 192 MiB of HBM per device.

```python
import math
import jax
import jax.numpy as jnp
from jax import lax

BLOCK = 128
NZ = 12
NBG = 16
NB = 64
SLOT = 2
NS = 16


def slot_order(subkey):
    return jax.random.permutation(subkey, NBG)


def offset_order(subkey):
    return jax.random.permutation(subkey, NS - 1)


def make_layout(key):
    base_key = jax.random.fold_in(key, 17)
    key_groups, key_slots, key_cycle, key_picks = jax.random.split(base_key, 4)
    groups = NB // NBG
    shuffle = jax.random.permutation(key_groups, groups).astype(jnp.int32)
    slot_values = jax.vmap(slot_order)(jax.random.split(key_slots, groups)).astype(jnp.int32)
    source = jnp.arange(groups, dtype=jnp.int32)[:, None]
    target = shuffle[(source + slot_values // 2) % groups]
    sort_key = (target * NB + source * NBG + slot_values).reshape(-1)
    ordering = jnp.argsort(sort_key)
    position = jnp.argsort(ordering).astype(jnp.int32)
    cycle_place = jax.random.permutation(key_cycle, NB).astype(jnp.int32)
    cycle_atoms = jnp.argsort(cycle_place).astype(jnp.int32)
    offsets = jnp.arange(NS, dtype=jnp.int32)
    places = (cycle_place[:, None] - NS // 2 + 1 + offsets[None, :]) % NB
    columns = cycle_atoms[places]
    ranking = jax.vmap(offset_order)(jax.random.split(key_picks, NB)).astype(jnp.int32)
    lookup = jnp.where(offsets < NS // 2 - 1, offsets, offsets - 1)
    lookup = jnp.clip(lookup, 0, NS - 2)
    chosen = (jnp.take(ranking, lookup, axis=1) < NZ - 1) | (offsets == NS // 2 - 1)[None, :]
    col_groups = NS // SLOT
    slot_index = places % col_groups * SLOT + offsets[None, :] // col_groups
    values = jnp.where(chosen, columns, -1).astype(jnp.int32)
    row_numbers = jnp.arange(NB, dtype=jnp.int32)[:, None]
    pattern = jnp.full((NB, NS), -1, jnp.int32).at[row_numbers, slot_index].set(values)
    return (position, pattern)


def draw_grid_position(key, part):
    return make_layout(key)[0]


def draw_pattern(key, part):
    return make_layout(key)[1]


def block_scale(rng, extent, pieces, smallest, high):
    def one(axis_at, blocks):
        heights = jax.random.uniform(jax.random.fold_in(jax.random.fold_in(rng, 6), axis_at), (blocks,), jnp.float32, smallest / len(pieces), high / len(pieces))
        return jnp.repeat(jnp.exp(heights), extent[axis_at] // blocks).reshape((-1,) + (1,) * (len(extent) - axis_at - 1))

    level = one(*pieces[0])
    for cut in pieces[1:]:
        level = level * one(*cut)
    return level


def bell_draw(rng, shape, width, bound, pieces=(), held_as=jnp.bfloat16):
    drawn = width * jax.random.normal(rng, shape, jnp.float32)
    if pieces:
        drawn = drawn * block_scale(rng, shape, pieces, -0.22, 0.18)
    return jnp.clip(drawn, -bound, bound).astype(held_as)


def setup_inputs(seed: int = 0) -> dict:
    arg_keys = jax.random.split(jax.random.key(seed), 4)
    return {
        "atom_blocks": bell_draw(arg_keys[0], (NB, NS, BLOCK, BLOCK), 1.0, 6.0, ((0, 4), (1, 8)), jnp.float32),
        "grid_position": draw_grid_position(jax.random.fold_in(arg_keys[3], 71), 0),
        "pattern": draw_pattern(jax.random.fold_in(arg_keys[3], 71), 0),
    }


HIGHEST = lax.Precision.HIGHEST

def restrict(left, right, pattern):

    def row_product(inputs):
        row_blocks, row_columns = inputs
        row_filled = row_columns >= 0
        neighbours = jnp.maximum(row_columns, 0)
        right_rows = right[neighbours]
        right_columns = pattern[neighbours]
        matches = (right_columns[:, :, None] == row_columns[None, None, :]) & row_filled[None, None, :] & row_filled[:, None, None]
        weights = jnp.einsum('uvt,uvpq->utpq', matches.astype(right.dtype), right_rows, precision=HIGHEST)
        return jnp.einsum('upq,utqr->tpr', row_blocks, weights, precision=HIGHEST)
    return lax.map(row_product, (left, pattern))

def reference(atom_blocks, grid_position, pattern):
    start_scale = 1.0 / math.sqrt(NZ * BLOCK)
    scale_back = math.sqrt(NZ * BLOCK)
    filled = (pattern >= 0)[:, :, None, None]
    matrix = jnp.where(filled, atom_blocks * start_scale, 0.0)
    masked_square = restrict(matrix, matrix, pattern)
    cubic = restrict(matrix, masked_square, pattern)
    square_atoms = masked_square * scale_back
    update_atoms = (1.5 * matrix - 0.5 * cubic) * scale_back
    square = jnp.zeros_like(square_atoms).at[grid_position].set(square_atoms)
    update = jnp.zeros_like(update_atoms).at[grid_position].set(update_atoms)
    return (square, update)
```

```python
import functools
import math

import jax
import jax.numpy as jnp
from jax import lax
from jax.experimental import pallas as pl
from jax.experimental.pallas import tpu as pltpu
from jax.sharding import PartitionSpec as P

NZ = 12
MESH = pl.DeviceIdType.MESH


def tables(grid_position, pattern, group_rows, slots, row_count, row_index, column_index):
    blocks = grid_position.shape[0]
    capacity = group_rows // row_count
    local = jnp.arange(group_rows, dtype=jnp.int32)
    target = (grid_position // group_rows).reshape(row_count, group_rows)
    earlier = (target[:, :, None] == target[:, None, :]) & (local[None, None, :] < local[None, :, None])
    rank = target * capacity + jnp.sum(earlier, axis=2, dtype=jnp.int32)
    panel_row = (rank + jnp.arange(row_count, dtype=jnp.int32)[:, None] * group_rows).reshape(-1)
    atoms = jnp.arange(blocks, dtype=jnp.int32)

    own_rows = row_index * group_rows + local
    atom_of_place = jnp.sum(jnp.where(panel_row[None, :] == own_rows[:, None], atoms[None, :], 0), axis=1)
    order = atom_of_place - row_index * group_rows
    is_atom = atom_of_place[:, None] == atoms[None, :]
    own_pattern = jnp.sum(jnp.where(is_atom[:, :, None], pattern[None], 0), axis=1)
    mine = lax.dynamic_slice_in_dim(own_pattern, column_index * slots, slots, 1)
    column_pattern = lax.dynamic_slice_in_dim(pattern, column_index * slots, slots, 1)
    is_neighbour = own_pattern[:, :, None] == atoms[None, None, :]
    zero_block = blocks * slots
    index = jnp.full((group_rows, own_pattern.shape[1], slots), zero_block, jnp.int32)
    for v in range(slots):
        wanted = column_pattern[None, None, :, v, None] == mine[:, None, None, :]
        hit = is_neighbour[:, :, :, None] & wanted & (mine >= 0)[:, None, None, :]
        place = (panel_row * slots + v)[None, None, :, None]
        index = index + jnp.sum(jnp.where(hit, place - zero_block, 0), axis=2)

    is_grid = grid_position[None, :] == own_rows[:, None]
    square_row = jnp.sum(jnp.where(is_grid, panel_row[None, :], 0), axis=1)
    source = square_row // group_rows
    update_row = source * capacity + square_row % group_rows - row_index * capacity
    filled = (mine >= 0).astype(jnp.float32)
    return order, index.reshape(-1), square_row, update_row, filled.reshape(-1)


def halves(x):
    high = x.astype(jnp.bfloat16)
    low = (x - high.astype(jnp.float32)).astype(jnp.bfloat16)
    return high, low


def kernel(
    row_count, chips, chunks,
    order_ref, index_ref, square_row_ref, update_row_ref, filled_ref, blocks_ref,
    square_ref, update_ref,
    left, right, square_panel, outgoing, incoming,
    left_send, left_recv, right_send, right_recv, panel_send, panel_recv, update_send, update_recv,
):
    group_rows, slots, edge = blocks_ref.shape[0], blocks_ref.shape[1], blocks_ref.shape[2]
    columns = 2 * chips
    capacity = group_rows // row_count
    height = group_rows // chunks
    grid_mesh = row_count == 4
    r = lax.axis_index("row")
    c = lax.axis_index("col")
    z = c // 2
    core = c % 2
    sibling = z * 2 + 1 - core
    x_side = r + 1 - 2 * (r % 2)
    y_side = lax.rem(r + 2, 4)
    start_scale = 1.0 / math.sqrt(NZ * edge)

    barrier = pltpu.get_barrier_semaphore()

    def greet(row, col):
        pl.semaphore_signal(barrier, inc=1, device_id=(row, col), device_id_type=MESH)

    greet(r, sibling)
    for d in range(1, row_count):
        greet(lax.rem(r + d, row_count), c)

    @pl.when(z > 0)
    def _():
        greet(r, c - 2)

    @pl.when(z < chips - 1)
    def _():
        greet(r, c + 2)

    zero_block = group_rows * row_count * slots
    right[zero_block] = jnp.zeros((edge, edge), jnp.float32)
    square_panel[zero_block] = jnp.zeros((edge, edge), jnp.float32)

    def bring(q, carry):
        row = blocks_ref[order_ref[q]]
        left[c, q] = row
        for s in range(slots):
            right[(r * group_rows + q) * slots + s] = row[s]
        return carry

    lax.fori_loop(0, group_rows, bring, 0)

    has_lower = (z + chips - 1) // chips
    has_upper = 1 - z // (chips - 1)
    pl.semaphore_wait(barrier, row_count + has_lower + has_upper)

    def part_copy(panel, send, recv, rows, source, part, way, target):
        span = panel.at[pl.ds((source * group_rows + part * rows) * slots, rows * slots)]
        return pltpu.make_async_remote_copy(
            src_ref=span, dst_ref=span, send_sem=send.at[way, part], recv_sem=recv.at[source, part],
            device_id=(target, c), device_id_type=MESH,
        )

    def part_wait(panel, send, recv, rows, source, part):
        part_copy(panel, send, recv, rows, source, part, 0, lax.rem(r + 1, row_count)).wait_recv()

    def spread(panel, send, recv, rows, first):
        if grid_mesh:
            for part, way in ((0, 0), (1, 1), (1, 0), (0, 1)):
                target = x_side if way == 0 else y_side
                part_copy(panel, send, recv, rows, r, first + part, way, target).start()
        else:
            for part in (0, 1):
                for d in range(1, row_count):
                    part_copy(panel, send, recv, rows, r, first + part, d - 1, lax.rem(r + d, row_count)).start()

    def pass_on(panel, send, recv, rows, first):
        if grid_mesh:
            part_wait(panel, send, recv, rows, x_side, first)
            part_copy(panel, send, recv, rows, x_side, first, 2, y_side).start()
            part_wait(panel, send, recv, rows, y_side, first + 1)
            part_copy(panel, send, recv, rows, y_side, first + 1, 3, x_side).start()

    def gather_rest(panel, send, recv, rows, first):
        if grid_mesh:
            part_wait(panel, send, recv, rows, x_side, first + 1)
            part_wait(panel, send, recv, rows, y_side, first)
            part_wait(panel, send, recv, rows, 3 - r, first)
            part_wait(panel, send, recv, rows, 3 - r, first + 1)
        else:
            for part in (0, 1):
                for d in range(1, row_count):
                    part_wait(panel, send, recv, rows, lax.rem(r + d, row_count), first + part)

    def sent(panel, send, recv, rows, first):
        if grid_mesh:
            ways = ((0, 0), (1, 0), (0, 1), (1, 1), (0, 2), (1, 3))
        else:
            ways = [(part, d) for part in (0, 1) for d in range(row_count - 1)]
        for part, way in ways:
            part_copy(panel, send, recv, rows, r, first + part, way, lax.rem(r + 1, row_count)).wait_send()

    matrix_side = (right, right_send, right_recv, group_rows // 2)
    square_side = (square_panel, panel_send, panel_recv, height // 2)

    def left_copy(source, chunk, way, target):
        span = left.at[source, pl.ds(chunk * height, height)]
        return pltpu.make_async_remote_copy(
            src_ref=span, dst_ref=span, send_sem=left_send.at[way, source, chunk],
            recv_sem=left_recv.at[source, chunk], device_id=(r, target), device_id_type=MESH,
        )

    def own_left(chunk):
        @pl.when(z < chips - 1)
        def _():
            left_copy(c, chunk, 0, c + 2).start()

        @pl.when(z > 0)
        def _():
            left_copy(c, chunk, 1, c - 2).start()

        left_copy(c, chunk, 2, sibling).start()

    def advance(chunk):
        @pl.when(chunk + 1 < chunks)
        def _():
            own_left(chunk + 1)

        for d in range(1, chips):
            @pl.when(z - d >= 0)
            def _():
                source = c - 2 * d
                left_copy(source, chunk, 0, sibling).wait_recv()

                @pl.when(z < chips - 1)
                def _():
                    left_copy(source, chunk, 0, c + 2).start()

                left_copy(source, chunk, 2, sibling).start()

            @pl.when(z + d < chips)
            def _():
                source = c + 2 * d
                left_copy(source, chunk, 0, sibling).wait_recv()

                @pl.when(z > 0)
                def _():
                    left_copy(source, chunk, 1, c - 2).start()

                left_copy(source, chunk, 2, sibling).start()

    def left_rest(chunk):
        def one(p, carry):
            left_copy(2 * p + 1 - core, chunk, 0, sibling).wait_recv()
            return carry

        lax.fori_loop(0, chips, one, 0)

    def left_sent(chunk, carry):
        def one(p, carry):
            source = 2 * p + core

            @pl.when((p <= z) & (z < chips - 1))
            def _():
                left_copy(source, chunk, 0, sibling).wait_send()

            @pl.when((p >= z) & (z > 0))
            def _():
                left_copy(source, chunk, 1, sibling).wait_send()

            left_copy(source, chunk, 2, sibling).wait_send()
            return carry

        lax.fori_loop(0, chips, one, 0)
        return carry

    def product(q, panel):
        total = jnp.zeros((edge, slots * edge), jnp.float32)
        for p in range(columns):
            row = left[p, q]
            a_high, a_low = halves(jnp.concatenate([row[u] for u in range(slots)], axis=1))
            b = jnp.concatenate(
                [
                    jnp.concatenate(
                        [panel[index_ref[((q * columns + p) * slots + u) * slots + t]] for t in range(slots)], axis=1
                    )
                    for u in range(slots)
                ],
                axis=0,
            )
            b_high, b_low = halves(b)
            total += jnp.dot(a_high, b_high, preferred_element_type=jnp.float32)
            total += jnp.dot(a_high, b_low, preferred_element_type=jnp.float32)
            total += jnp.dot(a_low, b_high, preferred_element_type=jnp.float32)
        return total

    def square_chunk(chunk):
        left_rest(chunk)

        def one(k, carry):
            q = chunk * height + k
            total = product(q, right) * start_scale
            for t in range(slots):
                square_panel[(r * group_rows + q) * slots + t] = total[:, t * edge : (t + 1) * edge]
            return carry

        lax.fori_loop(0, height, one, 0)
        spread(*square_side, 2 * chunk)

    half = chunks // 2
    spread(*matrix_side, 0)
    own_left(0)
    lax.fori_loop(0, half // 2, lambda h, carry: (advance(h), carry)[1], 0)
    pass_on(*matrix_side, 0)
    lax.fori_loop(half // 2, half, lambda h, carry: (advance(h), carry)[1], 0)
    gather_rest(*matrix_side, 0)

    def second(k, carry):
        advance(half + k)

        @pl.when(k > 0)
        def _():
            pass_on(*square_side, 4 * k - 4)
            pass_on(*square_side, 4 * k - 2)

        square_chunk(2 * k)
        square_chunk(2 * k + 1)
        return carry

    lax.fori_loop(0, half, second, 0)
    pass_on(*square_side, 4 * half - 4)
    pass_on(*square_side, 4 * half - 2)

    def rest(chunk, carry):
        gather_rest(*square_side, 2 * chunk)
        return carry

    lax.fori_loop(0, chunks, rest, 0)

    def update_rows(target, store):
        def one(k, carry):
            q = target * capacity + k
            total = product(q, square_panel) * (0.5 * start_scale)
            for t in range(slots):
                own = left[c, q, t] * (1.5 * filled_ref[q * slots + t])
                store(k, t, own - total[:, t * edge : (t + 1) * edge])
            return carry

        lax.fori_loop(0, capacity, one, 0)

    ways = [row_count - 1] + list(range(1, row_count - 1)) if not grid_mesh else [3, 1, 2]
    def target_of(way):
        if not grid_mesh:
            return lax.rem(r + way, row_count)
        return {1: x_side, 2: y_side, 3: 3 - r}[way]

    for way in ways:
        target = target_of(way)

        def store(k, t, value):
            outgoing[target * capacity + k, t] = value

        update_rows(target, store)
        pltpu.make_async_remote_copy(
            src_ref=outgoing.at[pl.ds(target * capacity, capacity)],
            dst_ref=incoming.at[pl.ds(r * capacity, capacity)],
            send_sem=update_send.at[way], recv_sem=update_recv.at[r],
            device_id=(target, c), device_id_type=MESH,
        ).start()

    def keep(k, t, value):
        incoming[r * capacity + k, t] = value

    update_rows(r, keep)

    def square_out(p, carry):
        row = square_row_ref[p]
        for t in range(slots):
            square_ref[p, t] = square_panel[row * slots + t]
        return carry

    lax.fori_loop(0, group_rows, square_out, 0)

    for way in ways:
        source = target_of(way) if grid_mesh else lax.rem(r + row_count - way, row_count)
        pltpu.make_async_remote_copy(
            src_ref=outgoing.at[pl.ds(0, capacity)],
            dst_ref=incoming.at[pl.ds(source * capacity, capacity)],
            send_sem=update_send.at[way], recv_sem=update_recv.at[source],
            device_id=(lax.rem(r + 1, row_count), c), device_id_type=MESH,
        ).wait()

    def update_out(p, carry):
        update_ref[p] = incoming[update_row_ref[p]]
        return carry

    lax.fori_loop(0, group_rows, update_out, 0)

    sent(*matrix_side, 0)

    def all_sent(chunk, carry):
        sent(*square_side, 2 * chunk)
        return carry

    lax.fori_loop(0, chunks, all_sent, 0)
    lax.fori_loop(0, chunks, left_sent, 0)


def on_device(atom_blocks, grid_position, pattern):
    group_rows, slots, edge = atom_blocks.shape[:3]
    row_count, columns = lax.axis_size("row"), lax.axis_size("col")
    chips = columns // 2
    chunks = 8
    order, index, square_row, update_row, filled = tables(
        grid_position, pattern, group_rows, slots, row_count, lax.axis_index("row"), lax.axis_index("col")
    )
    panel = (group_rows * row_count * slots + 1, edge, edge)
    ways = max(row_count, 4)
    smem = pl.BlockSpec(memory_space=pltpu.SMEM)
    vmem = pl.BlockSpec(memory_space=pltpu.VMEM)
    dma = pltpu.SemaphoreType.DMA
    out = jax.ShapeDtypeStruct(atom_blocks.shape, jnp.float32)
    return pl.pallas_call(
        functools.partial(kernel, row_count, chips, chunks),
        out_shape=(out, out),
        in_specs=[smem] * 5 + [vmem],
        out_specs=(vmem, vmem),
        scratch_shapes=[
            pltpu.VMEM((columns, group_rows, slots, edge, edge), jnp.float32),
            pltpu.VMEM(panel, jnp.float32),
            pltpu.VMEM(panel, jnp.float32),
            pltpu.VMEM((group_rows, slots, edge, edge), jnp.float32),
            pltpu.VMEM((group_rows, slots, edge, edge), jnp.float32),
            dma((3, columns, chunks)),
            dma((columns, chunks)),
            dma((ways, 2)),
            dma((row_count, 2)),
            dma((ways, 2 * chunks)),
            dma((row_count, 2 * chunks)),
            dma((ways,)),
            dma((row_count,)),
        ],
        compiler_params=pltpu.CompilerParams(
            collective_id=0, has_side_effects=True, vmem_limit_bytes=56 * 2**20
        ),
        cost_estimate=pl.CostEstimate(
            flops=12 * group_rows * columns * slots * slots * edge**3,
            bytes_accessed=12 * group_rows * slots * edge * edge,
            transcendentals=0,
        ),
    )(order, index, square_row, update_row, filled, atom_blocks)


def solution(mesh):
    in_specs = (P("row", "col", None, None), P(), P())
    out_specs = (P("row", "col", None, None), P("row", "col", None, None))
    return jax.shard_map(
        on_device, mesh=mesh, in_specs=in_specs, out_specs=out_specs, check_vma=False
    )
```

```python
import functools
import math

import jax
import jax.numpy as jnp
from jax import lax
from jax.experimental import pallas as pl
from jax.experimental.pallas import tpu as pltpu
from jax.sharding import PartitionSpec as P

NZ = 12
MESH = pl.DeviceIdType.MESH


def halves(x):
    high = x.astype(jnp.bfloat16)
    low = (x - high.astype(jnp.float32)).astype(jnp.bfloat16)
    return high, low


def kernel(
    row_count, chips, chunks,
    place_ref, pattern_ref, blocks_ref,
    square_ref, update_ref,
    left, right, square_panel, square_high, square_low, outgoing, incoming,
    index_ref, order_ref, square_row_ref, update_row_ref,
    left_send, left_recv, right_send, right_recv, panel_send, panel_recv, update_send, update_recv,
):
    group_rows, slots, edge = blocks_ref.shape[0], blocks_ref.shape[1], blocks_ref.shape[2]
    columns = 2 * chips
    capacity = group_rows // row_count
    height = group_rows // chunks
    all_slots = columns * slots
    grid_mesh = row_count == 4
    r = lax.axis_index("row")
    c = lax.axis_index("col")
    z = c // 2
    core = c % 2
    sibling = z * 2 + 1 - core
    x_side = r + 1 - 2 * (r % 2)
    y_side = lax.rem(r + 2, 4)
    start_scale = 1.0 / math.sqrt(NZ * edge)

    barrier = pltpu.get_barrier_semaphore()

    def greet(row, col):
        pl.semaphore_signal(barrier, inc=1, device_id=(row, col), device_id_type=MESH)

    greet(r, sibling)
    for d in range(1, row_count):
        greet(lax.rem(r + d, row_count), c)

    @pl.when(z > 0)
    def _():
        greet(r, c - 2)

    @pl.when(z < chips - 1)
    def _():
        greet(r, c + 2)

    zero_block = group_rows * row_count * slots
    right[zero_block] = jnp.zeros((edge, edge), jnp.float32)
    square_high[zero_block] = jnp.zeros((edge, edge), jnp.bfloat16)
    square_low[zero_block] = jnp.zeros((edge, edge), jnp.bfloat16)

    def bring(q, carry):
        row = blocks_ref[q]
        left[c, q] = row
        for s in range(slots):
            right[(r * group_rows + q) * slots + s] = row[s]
        return carry

    lax.fori_loop(0, group_rows, bring, 0)

    has_lower = (z + chips - 1) // chips
    has_upper = 1 - z // (chips - 1)
    pl.semaphore_wait(barrier, row_count + has_lower + has_upper)

    def part_copy(panel, send, recv, size, source, part, way, target):
        span = panel.at[pl.ds(source * group_rows * slots + part * size, size)]
        return pltpu.make_async_remote_copy(
            src_ref=span, dst_ref=span, send_sem=send.at[way, part], recv_sem=recv.at[source, part],
            device_id=(target, c), device_id_type=MESH,
        )

    def part_wait(panel, send, recv, size, source, part):
        part_copy(panel, send, recv, size, source, part, 0, lax.rem(r + 1, row_count)).wait_recv()

    def spread(panel, send, recv, size, first, turn):
        if grid_mesh:
            for part, way in ((0, 0), (1, 1)) if turn == 0 else ((1, 0), (0, 1)):
                target = x_side if way == 0 else y_side
                part_copy(panel, send, recv, size, r, first + part, way, target).start()
        else:
            for d in range(1, row_count):
                part_copy(panel, send, recv, size, r, first + turn, d - 1, lax.rem(r + d, row_count)).start()

    def pass_on(panel, send, recv, size, first):
        if grid_mesh:
            part_wait(panel, send, recv, size, x_side, first)
            part_copy(panel, send, recv, size, x_side, first, 2, y_side).start()
            part_wait(panel, send, recv, size, y_side, first + 1)
            part_copy(panel, send, recv, size, y_side, first + 1, 3, x_side).start()

    def gather_rest(panel, send, recv, size, first):
        if grid_mesh:
            part_wait(panel, send, recv, size, x_side, first + 1)
            part_wait(panel, send, recv, size, y_side, first)
            part_wait(panel, send, recv, size, 3 - r, first)
            part_wait(panel, send, recv, size, 3 - r, first + 1)
        else:
            for part in (0, 1):
                for d in range(1, row_count):
                    part_wait(panel, send, recv, size, lax.rem(r + d, row_count), first + part)

    def sent(panel, send, recv, size, first):
        if grid_mesh:
            ways = ((0, 0), (1, 0), (0, 1), (1, 1), (0, 2), (1, 3))
        else:
            ways = [(part, d) for part in (0, 1) for d in range(row_count - 1)]
        for part, way in ways:
            part_copy(panel, send, recv, size, r, first + part, way, lax.rem(r + 1, row_count)).wait_send()

    matrix_side = (right, right_send, right_recv, group_rows * slots // 2)
    square_side = (square_panel, panel_send, panel_recv, height * slots // 2)

    def left_copy(source, chunk, way, target):
        span = left.at[source, pl.ds(chunk * height, height)]
        return pltpu.make_async_remote_copy(
            src_ref=span, dst_ref=span, send_sem=left_send.at[way, source, chunk],
            recv_sem=left_recv.at[source, chunk], device_id=(r, target), device_id_type=MESH,
        )

    def own_left(chunk):
        @pl.when(z < chips - 1)
        def _():
            left_copy(c, chunk, 0, c + 2).start()

        @pl.when(z > 0)
        def _():
            left_copy(c, chunk, 1, c - 2).start()

        left_copy(c, chunk, 2, sibling).start()

    def advance(chunk):
        @pl.when(chunk + 1 < chunks)
        def _():
            own_left(chunk + 1)

        for d in range(1, chips):
            @pl.when(z - d >= 0)
            def _():
                source = c - 2 * d
                left_copy(source, chunk, 0, sibling).wait_recv()

                @pl.when(z < chips - 1)
                def _():
                    left_copy(source, chunk, 0, c + 2).start()

                left_copy(source, chunk, 2, sibling).start()

            @pl.when(z + d < chips)
            def _():
                source = c + 2 * d
                left_copy(source, chunk, 0, sibling).wait_recv()

                @pl.when(z > 0)
                def _():
                    left_copy(source, chunk, 1, c - 2).start()

                left_copy(source, chunk, 2, sibling).start()

    def left_rest(chunk):
        def one(p, carry):
            left_copy(2 * p + 1 - core, chunk, 0, sibling).wait_recv()
            return carry

        lax.fori_loop(0, chips, one, 0)

    def left_sent(chunk, carry):
        def one(p, carry):
            source = 2 * p + core

            @pl.when((p <= z) & (z < chips - 1))
            def _():
                left_copy(source, chunk, 0, sibling).wait_send()

            @pl.when((p >= z) & (z > 0))
            def _():
                left_copy(source, chunk, 1, sibling).wait_send()

            left_copy(source, chunk, 2, sibling).wait_send()
            return carry

        lax.fori_loop(0, chips, one, 0)
        return carry

    def make_index(q, carry):
        atom = r * group_rows + q
        wanted = [pattern_ref[atom * all_slots + c * slots + t] for t in range(slots)]
        for u in range(all_slots):
            neighbour = pattern_ref[atom * all_slots + u]
            at = jnp.maximum(neighbour, 0)
            held = [pattern_ref[at * all_slots + c * slots + v] for v in range(slots)]
            for t in range(slots):
                place = zero_block
                for v in range(slots):
                    place = jnp.where(held[v] == wanted[t], at * slots + v, place)
                place = jnp.where((neighbour >= 0) & (wanted[t] >= 0), place, zero_block)
                index_ref[(q * all_slots + u) * slots + t] = place
        return carry

    def make_order(place, carry):
        target, number = place // capacity, place % capacity
        found, count = jnp.int32(0), jnp.int32(0)
        for i in range(group_rows):
            hit = (place_ref[r * group_rows + i] // group_rows == target).astype(jnp.int32)
            found = jnp.where((hit == 1) & (count == number), i, found)
            count = count + hit
        order_ref[place] = found
        return carry

    def make_rows(p, carry):
        def look(a, found):
            return jnp.where(place_ref[a] == r * group_rows + p, a, found)

        atom = lax.fori_loop(0, row_count * group_rows, look, jnp.int32(0), unroll=8)
        source = atom // group_rows
        count = jnp.int32(0)
        for i in range(group_rows):
            hit = (place_ref[source * group_rows + i] // group_rows == r) & (i < atom % group_rows)
            count = count + hit.astype(jnp.int32)
        square_row_ref[p] = atom
        update_row_ref[p] = source * capacity + jnp.minimum(count, capacity - 1)
        return carry

    def product(q, panels):
        total = jnp.zeros((edge, slots * edge), jnp.float32)
        for p in range(columns):
            row = left[p, q]
            a_high, a_low = halves(jnp.concatenate([row[u] for u in range(slots)], axis=1))

            def weights(panel):
                return jnp.concatenate(
                    [
                        jnp.concatenate(
                            [panel[index_ref[(q * all_slots + p * slots + u) * slots + t]] for t in range(slots)],
                            axis=1,
                        )
                        for u in range(slots)
                    ],
                    axis=0,
                )

            if len(panels) == 1:
                b_high, b_low = halves(weights(panels[0]))
            else:
                b_high, b_low = weights(panels[0]), weights(panels[1])
            both = jnp.concatenate([a_high, a_low], axis=0)
            by_high = jnp.dot(both, b_high, preferred_element_type=jnp.float32)
            by_low = jnp.dot(a_high, b_low, preferred_element_type=jnp.float32)
            total = total + (by_high[:edge] + (by_high[edge:] + by_low))
        return total

    def square_chunk(chunk):
        left_rest(chunk)

        def one(k, carry):
            q = chunk * height + k
            total = product(q, (right,)) * start_scale
            for t in range(slots):
                square_panel[(r * group_rows + q) * slots + t] = total[:, t * edge : (t + 1) * edge]
            return carry

        lax.fori_loop(0, height, one, 0)
        spread(*square_side, 2 * chunk, 0)
        spread(*square_side, 2 * chunk, 1)

    def finish_chunk(chunk):
        gather_rest(*square_side, 2 * chunk)

        def one(source, carry):
            first = (source * group_rows + chunk * height) * slots
            for b in range(height * slots):
                high, low = halves(square_panel[first + b])
                square_high[first + b] = high
                square_low[first + b] = low
            return carry

        lax.fori_loop(0, row_count, one, 0)

    def advance_from(first, last):
        lax.fori_loop(first, last, lambda h, carry: (advance(h), carry)[1], 0)

    half = chunks // 2
    spread(*matrix_side, 0, 0)
    own_left(0)
    lax.fori_loop(0, group_rows, make_index, 0)
    advance_from(0, half // 4)
    spread(*matrix_side, 0, 1)
    lax.fori_loop(0, group_rows, make_order, 0)
    lax.fori_loop(0, group_rows, make_rows, 0)
    advance_from(half // 4, half // 2)
    pass_on(*matrix_side, 0)
    advance_from(half // 2, half)
    gather_rest(*matrix_side, 0)

    def second(k, carry):
        square_chunk(2 * k)
        advance(half + k)

        @pl.when(k > 0)
        def _():
            pass_on(*square_side, 4 * k - 4)
            pass_on(*square_side, 4 * k - 2)

        square_chunk(2 * k + 1)

        @pl.when(k > 1)
        def _():
            finish_chunk(2 * k - 4)
            finish_chunk(2 * k - 3)

        return carry

    lax.fori_loop(0, half, second, 0)
    pass_on(*square_side, 4 * half - 4)
    pass_on(*square_side, 4 * half - 2)
    lax.fori_loop(chunks - 4, chunks, lambda chunk, carry: (finish_chunk(chunk), carry)[1], 0)

    def update_rows(target, store):
        def one(k, carry):
            q = order_ref[target * capacity + k]
            total = product(q, (square_high, square_low)) * (0.5 * start_scale)
            for t in range(slots):
                filled = pattern_ref[(r * group_rows + q) * all_slots + c * slots + t] >= 0
                own = left[c, q, t] * jnp.where(filled, 1.5, 0.0)
                store(k, t, own - total[:, t * edge : (t + 1) * edge])
            return carry

        lax.fori_loop(0, capacity, one, 0)

    ways = [row_count - 1] + list(range(1, row_count - 1)) if not grid_mesh else [3, 1, 2]
    def target_of(way):
        if not grid_mesh:
            return lax.rem(r + way, row_count)
        return {1: x_side, 2: y_side, 3: 3 - r}[way]

    for way in ways:
        target = target_of(way)

        def store(k, t, value):
            outgoing[target * capacity + k, t] = value

        update_rows(target, store)
        pltpu.make_async_remote_copy(
            src_ref=outgoing.at[pl.ds(target * capacity, capacity)],
            dst_ref=incoming.at[pl.ds(r * capacity, capacity)],
            send_sem=update_send.at[way], recv_sem=update_recv.at[r],
            device_id=(target, c), device_id_type=MESH,
        ).start()

    def keep(k, t, value):
        incoming[r * capacity + k, t] = value

    update_rows(r, keep)

    def square_out(p, carry):
        row = square_row_ref[p]
        for t in range(slots):
            square_ref[p, t] = square_panel[row * slots + t]
        return carry

    lax.fori_loop(0, group_rows, square_out, 0)

    for way in ways:
        source = target_of(way) if grid_mesh else lax.rem(r + row_count - way, row_count)
        pltpu.make_async_remote_copy(
            src_ref=outgoing.at[pl.ds(0, capacity)],
            dst_ref=incoming.at[pl.ds(source * capacity, capacity)],
            send_sem=update_send.at[way], recv_sem=update_recv.at[source],
            device_id=(lax.rem(r + 1, row_count), c), device_id_type=MESH,
        ).wait()

    def update_out(p, carry):
        update_ref[p] = incoming[update_row_ref[p]]
        return carry

    lax.fori_loop(0, group_rows, update_out, 0)

    sent(*matrix_side, 0)

    def all_sent(chunk, carry):
        sent(*square_side, 2 * chunk)
        return carry

    lax.fori_loop(0, chunks, all_sent, 0)
    lax.fori_loop(0, chunks, left_sent, 0)


def on_device(atom_blocks, grid_position, pattern):
    group_rows, slots, edge = atom_blocks.shape[:3]
    row_count, columns = lax.axis_size("row"), lax.axis_size("col")
    chips = columns // 2
    chunks = group_rows * slots // 2
    panel = (group_rows * row_count * slots + 1, edge, edge)
    ways = max(row_count, 4)
    smem = pl.BlockSpec(memory_space=pltpu.SMEM)
    vmem = pl.BlockSpec(memory_space=pltpu.VMEM)
    dma = pltpu.SemaphoreType.DMA
    out = jax.ShapeDtypeStruct(atom_blocks.shape, jnp.float32)
    return pl.pallas_call(
        functools.partial(kernel, row_count, chips, chunks),
        out_shape=(out, out),
        in_specs=[smem] * 2 + [vmem],
        out_specs=(vmem, vmem),
        scratch_shapes=[
            pltpu.VMEM((columns, group_rows, slots, edge, edge), jnp.float32),
            pltpu.VMEM(panel, jnp.float32),
            pltpu.VMEM(panel, jnp.float32),
            pltpu.VMEM(panel, jnp.bfloat16),
            pltpu.VMEM(panel, jnp.bfloat16),
            pltpu.VMEM((group_rows, slots, edge, edge), jnp.float32),
            pltpu.VMEM((group_rows, slots, edge, edge), jnp.float32),
            pltpu.SMEM((group_rows * columns * slots * slots,), jnp.int32),
            pltpu.SMEM((group_rows,), jnp.int32),
            pltpu.SMEM((group_rows,), jnp.int32),
            pltpu.SMEM((group_rows,), jnp.int32),
            dma((3, columns, chunks)),
            dma((columns, chunks)),
            dma((ways, 2)),
            dma((row_count, 2)),
            dma((ways, 2 * chunks)),
            dma((row_count, 2 * chunks)),
            dma((ways,)),
            dma((row_count,)),
        ],
        compiler_params=pltpu.CompilerParams(
            collective_id=0, has_side_effects=True, vmem_limit_bytes=56 * 2**20
        ),
        cost_estimate=pl.CostEstimate(
            flops=12 * group_rows * columns * slots * slots * edge**3,
            bytes_accessed=12 * group_rows * slots * edge * edge,
            transcendentals=0,
        ),
    )(grid_position, pattern.reshape(-1), atom_blocks)


def solution(mesh):
    in_specs = (P("row", "col", None, None), P(), P())
    out_specs = (P("row", "col", None, None), P("row", "col", None, None))
    return jax.shard_map(
        on_device, mesh=mesh, in_specs=in_specs, out_specs=out_specs, check_vma=False
    )
```

```python
import functools
import math

import jax
import jax.numpy as jnp
from jax import lax
from jax.experimental import pallas as pl
from jax.experimental.pallas import tpu as pltpu
from jax.sharding import PartitionSpec as P

NZ = 12
MESH = pl.DeviceIdType.MESH


def halves(x):
    high = x.astype(jnp.bfloat16)
    low = (x - high.astype(jnp.float32)).astype(jnp.bfloat16)
    return high, low


def kernel(
    row_count, chips, chunks,
    place_ref, pattern_ref, blocks_ref,
    square_ref, update_ref,
    left, right, square_panel, square_high, square_low, outgoing, incoming,
    index_ref, order_ref, square_row_ref, update_row_ref,
    left_send, left_recv, right_send, right_recv, panel_send, panel_recv, update_send, update_recv,
):
    group_rows, slots, edge = blocks_ref.shape[0], blocks_ref.shape[1], blocks_ref.shape[2]
    columns = 2 * chips
    capacity = group_rows // row_count
    height = group_rows // chunks
    all_slots = columns * slots
    grid_mesh = row_count == 4
    r = lax.axis_index("row")
    c = lax.axis_index("col")
    z = c // 2
    core = c % 2
    sibling = z * 2 + 1 - core
    x_side = r + 1 - 2 * (r % 2)
    y_side = lax.rem(r + 2, 4)

    barrier = pltpu.get_barrier_semaphore()

    def greet(row, col):
        pl.semaphore_signal(barrier, inc=1, device_id=(row, col), device_id_type=MESH)

    greet(r, sibling)
    for d in range(1, row_count):
        greet(lax.rem(r + d, row_count), c)

    @pl.when(z > 0)
    def _():
        greet(r, c - 2)

    @pl.when(z < chips - 1)
    def _():
        greet(r, c + 2)

    zero_block = group_rows * row_count * slots
    right[zero_block] = jnp.zeros((edge, edge), jnp.float32)
    square_high[zero_block] = jnp.zeros((edge, edge), jnp.bfloat16)
    square_low[zero_block] = jnp.zeros((edge, edge), jnp.bfloat16)

    def bring(q, carry):
        row = blocks_ref[q]
        left[c, q] = row
        for s in range(slots):
            right[(r * group_rows + q) * slots + s] = row[s]
        return carry

    lax.fori_loop(0, group_rows, bring, 0)

    has_lower = (z + chips - 1) // chips
    has_upper = 1 - z // (chips - 1)
    middle = has_lower * has_upper
    pl.semaphore_wait(barrier, row_count + has_lower + has_upper)

    def part_copy(panel, send, recv, size, source, part, way, target):
        span = panel.at[pl.ds(source * group_rows * slots + part * size, size)]
        return pltpu.make_async_remote_copy(
            src_ref=span, dst_ref=span, send_sem=send.at[way, part], recv_sem=recv.at[source, part],
            device_id=(target, c), device_id_type=MESH,
        )

    def part_wait(panel, send, recv, size, source, part):
        part_copy(panel, send, recv, size, source, part, 0, lax.rem(r + 1, row_count)).wait_recv()

    def spread(panel, send, recv, size, first, turn):
        if grid_mesh:
            for part, way in ((0, 0), (1, 1)) if turn == 0 else ((1, 0), (0, 1)):
                target = x_side if way == 0 else y_side
                part_copy(panel, send, recv, size, r, first + part, way, target).start()
        else:
            for d in range(1, row_count):
                part_copy(panel, send, recv, size, r, first + turn, d - 1, lax.rem(r + d, row_count)).start()

    def pass_on(panel, send, recv, size, first):
        if grid_mesh:
            part_wait(panel, send, recv, size, x_side, first)
            part_copy(panel, send, recv, size, x_side, first, 2, y_side).start()
            part_wait(panel, send, recv, size, y_side, first + 1)
            part_copy(panel, send, recv, size, y_side, first + 1, 3, x_side).start()

    def gather_rest(panel, send, recv, size, first):
        if grid_mesh:
            part_wait(panel, send, recv, size, x_side, first + 1)
            part_wait(panel, send, recv, size, y_side, first)
            part_wait(panel, send, recv, size, 3 - r, first)
            part_wait(panel, send, recv, size, 3 - r, first + 1)
        else:
            for part in (0, 1):
                for d in range(1, row_count):
                    part_wait(panel, send, recv, size, lax.rem(r + d, row_count), first + part)

    def sent(panel, send, recv, size, first):
        if grid_mesh:
            ways = ((0, 0), (1, 0), (0, 1), (1, 1), (0, 2), (1, 3))
        else:
            ways = [(part, d) for part in (0, 1) for d in range(row_count - 1)]
        for part, way in ways:
            part_copy(panel, send, recv, size, r, first + part, way, lax.rem(r + 1, row_count)).wait_send()

    matrix_side = (right, right_send, right_recv, group_rows * slots // 2)
    square_side = (square_panel, panel_send, panel_recv, height * slots // 2)

    def left_copy(source, chunk, way, target):
        span = left.at[source, pl.ds(chunk * height, height)]
        return pltpu.make_async_remote_copy(
            src_ref=span, dst_ref=span, send_sem=left_send.at[way, source, chunk],
            recv_sem=left_recv.at[source, chunk], device_id=(r, target), device_id_type=MESH,
        )

    def own_left(chunk):
        @pl.when(z < chips - 1)
        def _():
            left_copy(c, chunk, 0, c + 2).start()

        @pl.when(z > 0)
        def _():
            left_copy(c, chunk, 1, c - 2).start()

        left_copy(c, chunk, 2, sibling).start()

    def advance(chunk):
        @pl.when((chunk + 1 < chunks) & (middle == 1))
        def _():
            own_left(chunk + 1)

        for d in range(1, chips):
            @pl.when(z - d >= 0)
            def _():
                source = c - 2 * d
                left_copy(source, chunk, 0, sibling).wait_recv()

                @pl.when(z < chips - 1)
                def _():
                    left_copy(source, chunk, 0, c + 2).start()

                left_copy(source, chunk, 2, sibling).start()

            @pl.when(z + d < chips)
            def _():
                source = c + 2 * d
                left_copy(source, chunk, 0, sibling).wait_recv()

                @pl.when(z > 0)
                def _():
                    left_copy(source, chunk, 1, c - 2).start()

                left_copy(source, chunk, 2, sibling).start()

    def left_rest(chunk):
        def one(p, carry):
            left_copy(2 * p + 1 - core, chunk, 0, sibling).wait_recv()
            return carry

        lax.fori_loop(0, chips, one, 0)

    def left_sent(chunk, carry):
        def one(p, carry):
            source = 2 * p + core

            @pl.when((p <= z) & (z < chips - 1))
            def _():
                left_copy(source, chunk, 0, sibling).wait_send()

            @pl.when((p >= z) & (z > 0))
            def _():
                left_copy(source, chunk, 1, sibling).wait_send()

            left_copy(source, chunk, 2, sibling).wait_send()
            return carry

        lax.fori_loop(0, chips, one, 0)
        return carry

    def make_index(q, carry):
        atom = r * group_rows + q
        wanted = [pattern_ref[atom, c * slots + t] for t in range(slots)]
        for u in range(all_slots):
            neighbour = pattern_ref[atom, u]
            at = jnp.maximum(neighbour, 0)
            held = [pattern_ref[at, c * slots + v] for v in range(slots)]
            for t in range(slots):
                place = zero_block
                for v in range(slots):
                    place = jnp.where(held[v] == wanted[t], at * slots + v, place)
                place = jnp.where((neighbour >= 0) & (wanted[t] >= 0), place, zero_block)
                index_ref[(q * all_slots + u) * slots + t] = place
        return carry

    def make_order(place, carry):
        target, number = place // capacity, place % capacity
        found, count = jnp.int32(0), jnp.int32(0)
        for i in range(group_rows):
            hit = (place_ref[r * group_rows + i] // group_rows == target).astype(jnp.int32)
            found = jnp.where((hit == 1) & (count == number), i, found)
            count = count + hit
        order_ref[place] = found
        return carry

    def make_rows(p, carry):
        def look(a, found):
            return jnp.where(place_ref[a] == r * group_rows + p, a, found)

        atom = lax.fori_loop(0, row_count * group_rows, look, jnp.int32(0), unroll=8)
        source = atom // group_rows
        count = jnp.int32(0)
        for i in range(group_rows):
            hit = (place_ref[source * group_rows + i] // group_rows == r) & (i < atom % group_rows)
            count = count + hit.astype(jnp.int32)
        square_row_ref[p] = atom
        update_row_ref[p] = source * capacity + jnp.minimum(count, capacity - 1)
        return carry

    def product(q, panels):
        total = jnp.zeros((edge, slots * edge), jnp.float32)
        for p in range(columns):
            row = left[p, q]
            a_high, a_low = halves(jnp.concatenate([row[u] for u in range(slots)], axis=1))

            def weights(panel):
                return jnp.concatenate(
                    [
                        jnp.concatenate(
                            [panel[index_ref[(q * all_slots + p * slots + u) * slots + t]] for t in range(slots)],
                            axis=1,
                        )
                        for u in range(slots)
                    ],
                    axis=0,
                )

            if len(panels) == 1:
                b_high, b_low = halves(weights(panels[0]))
            else:
                b_high, b_low = weights(panels[0]), weights(panels[1])
            both = jnp.concatenate([a_high, a_low], axis=0)
            by_high = jnp.dot(both, b_high, preferred_element_type=jnp.float32)
            by_low = jnp.dot(a_high, b_low, preferred_element_type=jnp.float32)
            total = total + (by_high[:edge] + (by_high[edge:] + by_low))
        return total

    def square_chunk(chunk):
        left_rest(chunk)

        def one(k, carry):
            q = chunk * height + k
            total = product(q, (right,))
            for t in range(slots):
                square_panel[(r * group_rows + q) * slots + t] = total[:, t * edge : (t + 1) * edge]
            return carry

        lax.fori_loop(0, height, one, 0)
        spread(*square_side, 2 * chunk, 0)
        spread(*square_side, 2 * chunk, 1)

    def finish_chunk(chunk):
        gather_rest(*square_side, 2 * chunk)

        def one(source, carry):
            first = (source * group_rows + chunk * height) * slots
            for b in range(height * slots):
                high, low = halves(square_panel[first + b])
                square_high[first + b] = high
                square_low[first + b] = low
            return carry

        lax.fori_loop(0, row_count, one, 0)

    def advance_from(first, last):
        lax.fori_loop(first, last, lambda h, carry: (advance(h), carry)[1], 0)

    half = chunks // 2
    quarter = half // 2
    lead = half + middle * (half - half * 3 // 8)
    spread(*matrix_side, 0, 0)
    own_left(0)

    @pl.when(middle == 0)
    def _():
        lax.fori_loop(1, chunks, lambda h, carry: (own_left(h), carry)[1], 0)

    lax.fori_loop(0, group_rows, make_index, 0)
    advance_from(0, half // 4)
    spread(*matrix_side, 0, 1)
    lax.fori_loop(0, group_rows, make_order, 0)
    lax.fori_loop(0, group_rows, make_rows, 0)
    advance_from(half // 4, quarter)
    pass_on(*matrix_side, 0)
    advance_from(quarter, half)
    advance_from(half, lead)
    gather_rest(*matrix_side, 0)
    lax.fori_loop(0, quarter, lambda m, carry: (square_chunk(m), carry)[1], 0)

    def advance_late(chunk):
        @pl.when(chunk >= lead)
        def _():
            advance(chunk)

    def second(k, carry):
        advance_late(half + k)
        pass_on(*square_side, 4 * k)
        pass_on(*square_side, 4 * k + 2)
        square_chunk(quarter + 2 * k)
        square_chunk(quarter + 2 * k + 1)

        @pl.when(k > 0)
        def _():
            finish_chunk(2 * k - 2)
            finish_chunk(2 * k - 1)

        return carry

    def third(k, carry):
        advance_late(half + quarter + k)
        square_chunk(half + quarter + k)

        @pl.when(k < quarter // 2)
        def _():
            pass_on(*square_side, 2 * (half + 2 * k))
            pass_on(*square_side, 2 * (half + 2 * k + 1))

        @pl.when(k >= quarter // 2)
        def _():
            pass_on(*square_side, 2 * (half + quarter // 2 + k))

        @pl.when(k <= quarter // 2)
        def _():
            finish_chunk(half - 2 + 2 * k)
            finish_chunk(half - 1 + 2 * k)

        return carry

    lax.fori_loop(0, quarter, second, 0)
    lax.fori_loop(0, quarter, third, 0)
    lax.fori_loop(
        half + quarter + quarter // 2, chunks, lambda m, carry: (pass_on(*square_side, 2 * m), carry)[1], 0
    )
    lax.fori_loop(half + quarter, chunks, lambda m, carry: (finish_chunk(m), carry)[1], 0)

    def update_rows(target, store):
        def one(k, carry):
            q = order_ref[target * capacity + k]
            total = product(q, (square_high, square_low)) * (1.0 / (NZ * edge))
            for t in range(slots):
                filled = pattern_ref[r * group_rows + q, c * slots + t] >= 0
                own = left[c, q, t] * jnp.where(filled, 3.0, 0.0)
                store(k, t, own - total[:, t * edge : (t + 1) * edge])
            return carry

        lax.fori_loop(0, capacity, one, 0)

    ways = [row_count - 1] + list(range(1, row_count - 1)) if not grid_mesh else [3, 1, 2]
    def target_of(way):
        if not grid_mesh:
            return lax.rem(r + way, row_count)
        return {1: x_side, 2: y_side, 3: 3 - r}[way]

    for way in ways:
        target = target_of(way)

        def store(k, t, value):
            outgoing[target * capacity + k, t] = value

        update_rows(target, store)
        pltpu.make_async_remote_copy(
            src_ref=outgoing.at[pl.ds(target * capacity, capacity)],
            dst_ref=incoming.at[pl.ds(r * capacity, capacity)],
            send_sem=update_send.at[way], recv_sem=update_recv.at[r],
            device_id=(target, c), device_id_type=MESH,
        ).start()

    def keep(k, t, value):
        incoming[r * capacity + k, t] = value

    update_rows(r, keep)

    def square_out(p, carry):
        row = square_row_ref[p]
        for t in range(slots):
            square_ref[p, t] = square_panel[row * slots + t]
        return carry

    lax.fori_loop(0, group_rows, square_out, 0)

    for way in ways:
        source = target_of(way) if grid_mesh else lax.rem(r + row_count - way, row_count)
        pltpu.make_async_remote_copy(
            src_ref=outgoing.at[pl.ds(0, capacity)],
            dst_ref=incoming.at[pl.ds(source * capacity, capacity)],
            send_sem=update_send.at[way], recv_sem=update_recv.at[source],
            device_id=(lax.rem(r + 1, row_count), c), device_id_type=MESH,
        ).wait()

    def update_out(p, carry):
        update_ref[p] = incoming[update_row_ref[p]]
        return carry

    lax.fori_loop(0, group_rows, update_out, 0)

    sent(*matrix_side, 0)

    def all_sent(chunk, carry):
        sent(*square_side, 2 * chunk)
        return carry

    lax.fori_loop(0, chunks, all_sent, 0)
    lax.fori_loop(0, chunks, left_sent, 0)


def on_device(atom_blocks, grid_position, pattern):
    group_rows, slots, edge = atom_blocks.shape[:3]
    row_count, columns = lax.axis_size("row"), lax.axis_size("col")
    chips = columns // 2
    chunks = group_rows * slots // 2
    panel = (group_rows * row_count * slots + 1, edge, edge)
    ways = max(row_count, 4)
    smem = pl.BlockSpec(memory_space=pltpu.SMEM)
    vmem = pl.BlockSpec(memory_space=pltpu.VMEM)
    dma = pltpu.SemaphoreType.DMA
    out = jax.ShapeDtypeStruct(atom_blocks.shape, jnp.float32)
    square, update = pl.pallas_call(
        functools.partial(kernel, row_count, chips, chunks),
        out_shape=(out, out),
        in_specs=[smem] * 2 + [vmem],
        out_specs=(vmem, vmem),
        scratch_shapes=[
            pltpu.VMEM((columns, group_rows, slots, edge, edge), jnp.float32),
            pltpu.VMEM(panel, jnp.float32),
            pltpu.VMEM(panel, jnp.float32),
            pltpu.VMEM(panel, jnp.bfloat16),
            pltpu.VMEM(panel, jnp.bfloat16),
            pltpu.VMEM((group_rows, slots, edge, edge), jnp.float32),
            pltpu.VMEM((group_rows, slots, edge, edge), jnp.float32),
            pltpu.SMEM((group_rows * columns * slots * slots,), jnp.int32),
            pltpu.SMEM((group_rows,), jnp.int32),
            pltpu.SMEM((group_rows,), jnp.int32),
            pltpu.SMEM((group_rows,), jnp.int32),
            dma((3, columns, chunks)),
            dma((columns, chunks)),
            dma((ways, 2)),
            dma((row_count, 2)),
            dma((ways, 2 * chunks)),
            dma((row_count, 2 * chunks)),
            dma((ways,)),
            dma((row_count,)),
        ],
        compiler_params=pltpu.CompilerParams(
            collective_id=0, has_side_effects=True, vmem_limit_bytes=56 * 2**20
        ),
        cost_estimate=pl.CostEstimate(
            flops=12 * group_rows * columns * slots * slots * edge**3,
            bytes_accessed=12 * group_rows * slots * edge * edge,
            transcendentals=0,
        ),
    )(grid_position, pattern, atom_blocks)
    return square * (1.0 / math.sqrt(NZ * edge)), update * 0.5


def solution(mesh):
    in_specs = (P("row", "col", None, None), P(), P())
    out_specs = (P("row", "col", None, None), P("row", "col", None, None))
    return jax.shard_map(
        on_device, mesh=mesh, in_specs=in_specs, out_specs=out_specs, check_vma=False
    )
```

```python
import functools
import math

import jax
import jax.numpy as jnp
from jax import lax
from jax.experimental import pallas as pl
from jax.experimental.pallas import tpu as pltpu
from jax.sharding import PartitionSpec as P

NZ = 12
MESH = pl.DeviceIdType.MESH


def halves(x):
    high = x.astype(jnp.bfloat16)
    low = (x - high.astype(jnp.float32)).astype(jnp.bfloat16)
    return high, low


def kernel(
    row_count, chips, chunks,
    place_ref, pattern_ref, blocks_ref,
    square_ref, update_ref,
    left, right, square_panel, square_high, square_low, outgoing, incoming,
    index_ref, order_ref, square_row_ref, update_row_ref,
    left_send, left_recv, right_send, right_recv, panel_send, panel_recv, update_send, update_recv,
):
    group_rows, slots, edge = blocks_ref.shape[0], blocks_ref.shape[1], blocks_ref.shape[2]
    columns = 2 * chips
    capacity = group_rows // row_count
    height = group_rows // chunks
    ahead = 3
    all_slots = columns * slots
    grid_mesh = row_count == 4
    r = lax.axis_index("row")
    c = lax.axis_index("col")
    z = c // 2
    core = c % 2
    sibling = z * 2 + 1 - core
    x_side = r + 1 - 2 * (r % 2)
    y_side = lax.rem(r + 2, 4)
    start_scale = 1.0 / math.sqrt(NZ * edge)

    barrier = pltpu.get_barrier_semaphore()

    def greet(row, col):
        pl.semaphore_signal(barrier, inc=1, device_id=(row, col), device_id_type=MESH)

    greet(r, sibling)
    for d in range(1, row_count):
        greet(lax.rem(r + d, row_count), c)

    @pl.when(z > 0)
    def _():
        greet(r, c - 2)

    @pl.when(z < chips - 1)
    def _():
        greet(r, c + 2)

    zero_block = group_rows * row_count * slots
    right[zero_block] = jnp.zeros((edge, edge), jnp.float32)
    square_high[zero_block] = jnp.zeros((edge, edge), jnp.bfloat16)
    square_low[zero_block] = jnp.zeros((edge, edge), jnp.bfloat16)

    def bring(q, carry):
        row = blocks_ref[q]
        left[c, q] = row
        for s in range(slots):
            right[(r * group_rows + q) * slots + s] = row[s]
        return carry

    lax.fori_loop(0, group_rows, bring, 0)

    has_lower = (z + chips - 1) // chips
    has_upper = 1 - z // (chips - 1)
    pl.semaphore_wait(barrier, row_count + has_lower + has_upper)

    def part_copy(panel, send, recv, size, source, part, way, target):
        span = panel.at[pl.ds(source * group_rows * slots + part * size, size)]
        return pltpu.make_async_remote_copy(
            src_ref=span, dst_ref=span, send_sem=send.at[way, part], recv_sem=recv.at[source, part],
            device_id=(target, c), device_id_type=MESH,
        )

    def part_wait(panel, send, recv, size, source, part):
        part_copy(panel, send, recv, size, source, part, 0, lax.rem(r + 1, row_count)).wait_recv()

    def spread(panel, send, recv, size, first, turn):
        if grid_mesh:
            for part, way in ((0, 0), (1, 1)) if turn == 0 else ((1, 0), (0, 1)):
                target = x_side if way == 0 else y_side
                part_copy(panel, send, recv, size, r, first + part, way, target).start()
        else:
            for d in range(1, row_count):
                part_copy(panel, send, recv, size, r, first + turn, d - 1, lax.rem(r + d, row_count)).start()

    def pass_on(panel, send, recv, size, first):
        if grid_mesh:
            part_wait(panel, send, recv, size, x_side, first)
            part_copy(panel, send, recv, size, x_side, first, 2, y_side).start()
            part_wait(panel, send, recv, size, y_side, first + 1)
            part_copy(panel, send, recv, size, y_side, first + 1, 3, x_side).start()

    def gather_rest(panel, send, recv, size, first):
        if grid_mesh:
            part_wait(panel, send, recv, size, x_side, first + 1)
            part_wait(panel, send, recv, size, y_side, first)
            part_wait(panel, send, recv, size, 3 - r, first)
            part_wait(panel, send, recv, size, 3 - r, first + 1)
        else:
            for part in (0, 1):
                for d in range(1, row_count):
                    part_wait(panel, send, recv, size, lax.rem(r + d, row_count), first + part)

    def sent(panel, send, recv, size, first):
        if grid_mesh:
            ways = ((0, 0), (1, 0), (0, 1), (1, 1), (0, 2), (1, 3))
        else:
            ways = [(part, d) for part in (0, 1) for d in range(row_count - 1)]
        for part, way in ways:
            part_copy(panel, send, recv, size, r, first + part, way, lax.rem(r + 1, row_count)).wait_send()

    matrix_side = (right, right_send, right_recv, group_rows * slots // chunks)
    square_side = (square_panel, panel_send, panel_recv, height * slots // 2)

    def left_copy(source, chunk, way, target):
        span = left.at[source, pl.ds(chunk * height, height)]
        return pltpu.make_async_remote_copy(
            src_ref=span, dst_ref=span, send_sem=left_send.at[way, source, chunk],
            recv_sem=left_recv.at[source, chunk], device_id=(r, target), device_id_type=MESH,
        )

    def own_left(chunk):
        @pl.when(z < chips - 1)
        def _():
            left_copy(c, chunk, 0, c + 2).start()

        @pl.when(z > 0)
        def _():
            left_copy(c, chunk, 1, c - 2).start()

        left_copy(c, chunk, 2, sibling).start()

    def advance(chunk):
        @pl.when(chunk + ahead < chunks)
        def _():
            own_left(chunk + ahead)

        for d in range(1, chips):
            @pl.when(z - d >= 0)
            def _():
                source = c - 2 * d
                left_copy(source, chunk, 0, sibling).wait_recv()

                @pl.when(z < chips - 1)
                def _():
                    left_copy(source, chunk, 0, c + 2).start()

                left_copy(source, chunk, 2, sibling).start()

            @pl.when(z + d < chips)
            def _():
                source = c + 2 * d
                left_copy(source, chunk, 0, sibling).wait_recv()

                @pl.when(z > 0)
                def _():
                    left_copy(source, chunk, 1, c - 2).start()

                left_copy(source, chunk, 2, sibling).start()

    def left_rest(chunk):
        def one(p, carry):
            left_copy(2 * p + 1 - core, chunk, 0, sibling).wait_recv()
            return carry

        lax.fori_loop(0, chips, one, 0)

    def left_sent(chunk, carry):
        def one(p, carry):
            source = 2 * p + core

            @pl.when((p <= z) & (z < chips - 1))
            def _():
                left_copy(source, chunk, 0, sibling).wait_send()

            @pl.when((p >= z) & (z > 0))
            def _():
                left_copy(source, chunk, 1, sibling).wait_send()

            left_copy(source, chunk, 2, sibling).wait_send()
            return carry

        lax.fori_loop(0, chips, one, 0)
        return carry

    def make_index(q, carry):
        atom = r * group_rows + q
        wanted = [pattern_ref[atom, c * slots + t] for t in range(slots)]
        for u in range(all_slots):
            neighbour = pattern_ref[atom, u]
            at = jnp.maximum(neighbour, 0)
            held = [pattern_ref[at, c * slots + v] for v in range(slots)]
            for t in range(slots):
                place = zero_block
                for v in range(slots):
                    place = jnp.where(held[v] == wanted[t], at * slots + v, place)
                place = jnp.where((neighbour >= 0) & (wanted[t] >= 0), place, zero_block)
                index_ref[(q * all_slots + u) * slots + t] = place
        return carry

    def make_order(place, carry):
        target, number = place // capacity, place % capacity
        found, count = jnp.int32(0), jnp.int32(0)
        for i in range(group_rows):
            hit = (place_ref[r * group_rows + i] // group_rows == target).astype(jnp.int32)
            found = jnp.where((hit == 1) & (count == number), i, found)
            count = count + hit
        order_ref[place] = found
        return carry

    def make_rows(p, carry):
        def look(a, found):
            return jnp.where(place_ref[a] == r * group_rows + p, a, found)

        atom = lax.fori_loop(0, row_count * group_rows, look, jnp.int32(0), unroll=8)
        source = atom // group_rows
        count = jnp.int32(0)
        for i in range(group_rows):
            hit = (place_ref[source * group_rows + i] // group_rows == r) & (i < atom % group_rows)
            count = count + hit.astype(jnp.int32)
        square_row_ref[p] = atom
        update_row_ref[p] = source * capacity + jnp.minimum(count, capacity - 1)
        return carry

    def product(q, panels):
        total = jnp.zeros((edge, slots * edge), jnp.float32)
        for p in range(columns):
            row = left[p, q]
            a_high, a_low = halves(jnp.concatenate([row[u] for u in range(slots)], axis=1))

            def weights(panel):
                return jnp.concatenate(
                    [
                        jnp.concatenate(
                            [panel[index_ref[(q * all_slots + p * slots + u) * slots + t]] for t in range(slots)],
                            axis=1,
                        )
                        for u in range(slots)
                    ],
                    axis=0,
                )

            if len(panels) == 1:
                b_high, b_low = halves(weights(panels[0]))
            else:
                b_high, b_low = weights(panels[0]), weights(panels[1])
            both = jnp.concatenate([a_high, a_low], axis=0)
            by_high = jnp.dot(both, b_high, preferred_element_type=jnp.float32)
            by_low = jnp.dot(a_high, b_low, preferred_element_type=jnp.float32)
            total = total + (by_high[:edge] + (by_high[edge:] + by_low))
        return total

    def square_chunk(chunk):
        left_rest(chunk)

        def one(k, carry):
            q = chunk * height + k
            total = product(q, (right,)) * start_scale
            for t in range(slots):
                square_panel[(r * group_rows + q) * slots + t] = total[:, t * edge : (t + 1) * edge]
            return carry

        lax.fori_loop(0, height, one, 0)
        spread(*square_side, 2 * chunk, 0)
        spread(*square_side, 2 * chunk, 1)

    def finish_chunk(chunk):
        gather_rest(*square_side, 2 * chunk)

        def one(source, carry):
            first = (source * group_rows + chunk * height) * slots
            for b in range(height * slots):
                high, low = halves(square_panel[first + b])
                square_high[first + b] = high
                square_low[first + b] = low
            return carry

        lax.fori_loop(0, row_count, one, 0)

    half = chunks // 2

    def spread_both(side, first):
        spread(*side, first, 0)
        spread(*side, first, 1)

    def step(h, carry):
        @pl.when(h + 2 < half)
        def _():
            spread_both(matrix_side, 2 * h + 4)

        advance(h)
        pass_on(*matrix_side, 2 * h)
        return carry

    own_left(0)
    spread_both(matrix_side, 0)
    own_left(1)
    spread_both(matrix_side, 2)
    own_left(2)
    lax.fori_loop(0, group_rows, make_index, 0)
    lax.fori_loop(0, half // 2, step, 0)
    lax.fori_loop(0, group_rows, make_order, 0)
    lax.fori_loop(0, group_rows, make_rows, 0)
    lax.fori_loop(half // 2, half, step, 0)
    lax.fori_loop(0, half, lambda h, carry: (gather_rest(*matrix_side, 2 * h), carry)[1], 0)

    def second(k, carry):
        square_chunk(2 * k)
        advance(half + k)

        @pl.when(k > 0)
        def _():
            pass_on(*square_side, 4 * k - 4)
            pass_on(*square_side, 4 * k - 2)

        square_chunk(2 * k + 1)

        @pl.when(k > 1)
        def _():
            finish_chunk(2 * k - 4)
            finish_chunk(2 * k - 3)

        return carry

    lax.fori_loop(0, half, second, 0)
    pass_on(*square_side, 4 * half - 4)
    pass_on(*square_side, 4 * half - 2)
    lax.fori_loop(chunks - 4, chunks, lambda chunk, carry: (finish_chunk(chunk), carry)[1], 0)

    def update_rows(target, store):
        def one(k, carry):
            q = order_ref[target * capacity + k]
            total = product(q, (square_high, square_low)) * (0.5 * start_scale)
            for t in range(slots):
                filled = pattern_ref[r * group_rows + q, c * slots + t] >= 0
                own = left[c, q, t] * jnp.where(filled, 1.5, 0.0)
                store(k, t, own - total[:, t * edge : (t + 1) * edge])
            return carry

        lax.fori_loop(0, capacity, one, 0)

    ways = [row_count - 1] + list(range(1, row_count - 1)) if not grid_mesh else [3, 1, 2]
    def target_of(way):
        if not grid_mesh:
            return lax.rem(r + way, row_count)
        return {1: x_side, 2: y_side, 3: 3 - r}[way]

    for way in ways:
        target = target_of(way)

        def store(k, t, value):
            outgoing[target * capacity + k, t] = value

        update_rows(target, store)
        pltpu.make_async_remote_copy(
            src_ref=outgoing.at[pl.ds(target * capacity, capacity)],
            dst_ref=incoming.at[pl.ds(r * capacity, capacity)],
            send_sem=update_send.at[way], recv_sem=update_recv.at[r],
            device_id=(target, c), device_id_type=MESH,
        ).start()

    def keep(k, t, value):
        incoming[r * capacity + k, t] = value

    update_rows(r, keep)

    def square_out(p, carry):
        row = square_row_ref[p]
        for t in range(slots):
            square_ref[p, t] = square_panel[row * slots + t]
        return carry

    lax.fori_loop(0, group_rows, square_out, 0)

    for way in ways:
        source = target_of(way) if grid_mesh else lax.rem(r + row_count - way, row_count)
        pltpu.make_async_remote_copy(
            src_ref=outgoing.at[pl.ds(0, capacity)],
            dst_ref=incoming.at[pl.ds(source * capacity, capacity)],
            send_sem=update_send.at[way], recv_sem=update_recv.at[source],
            device_id=(lax.rem(r + 1, row_count), c), device_id_type=MESH,
        ).wait()

    def update_out(p, carry):
        update_ref[p] = incoming[update_row_ref[p]]
        return carry

    lax.fori_loop(0, group_rows, update_out, 0)

    lax.fori_loop(0, half, lambda h, carry: (sent(*matrix_side, 2 * h), carry)[1], 0)

    def all_sent(chunk, carry):
        sent(*square_side, 2 * chunk)
        return carry

    lax.fori_loop(0, chunks, all_sent, 0)
    lax.fori_loop(0, chunks, left_sent, 0)


def on_device(atom_blocks, grid_position, pattern):
    group_rows, slots, edge = atom_blocks.shape[:3]
    row_count, columns = lax.axis_size("row"), lax.axis_size("col")
    chips = columns // 2
    chunks = group_rows * slots // 2
    panel = (group_rows * row_count * slots + 1, edge, edge)
    ways = max(row_count, 4)
    smem = pl.BlockSpec(memory_space=pltpu.SMEM)
    vmem = pl.BlockSpec(memory_space=pltpu.VMEM)
    dma = pltpu.SemaphoreType.DMA
    out = jax.ShapeDtypeStruct(atom_blocks.shape, jnp.float32)
    return pl.pallas_call(
        functools.partial(kernel, row_count, chips, chunks),
        out_shape=(out, out),
        in_specs=[smem] * 2 + [vmem],
        out_specs=(vmem, vmem),
        scratch_shapes=[
            pltpu.VMEM((columns, group_rows, slots, edge, edge), jnp.float32),
            pltpu.VMEM(panel, jnp.float32),
            pltpu.VMEM(panel, jnp.float32),
            pltpu.VMEM(panel, jnp.bfloat16),
            pltpu.VMEM(panel, jnp.bfloat16),
            pltpu.VMEM((group_rows, slots, edge, edge), jnp.float32),
            pltpu.VMEM((group_rows, slots, edge, edge), jnp.float32),
            pltpu.SMEM((group_rows * columns * slots * slots,), jnp.int32),
            pltpu.SMEM((group_rows,), jnp.int32),
            pltpu.SMEM((group_rows,), jnp.int32),
            pltpu.SMEM((group_rows,), jnp.int32),
            dma((3, columns, chunks)),
            dma((columns, chunks)),
            dma((ways, chunks)),
            dma((row_count, chunks)),
            dma((ways, 2 * chunks)),
            dma((row_count, 2 * chunks)),
            dma((ways,)),
            dma((row_count,)),
        ],
        compiler_params=pltpu.CompilerParams(
            collective_id=0, has_side_effects=True, vmem_limit_bytes=56 * 2**20
        ),
        cost_estimate=pl.CostEstimate(
            flops=12 * group_rows * columns * slots * slots * edge**3,
            bytes_accessed=12 * group_rows * slots * edge * edge,
            transcendentals=0,
        ),
    )(grid_position, pattern, atom_blocks)


def solution(mesh):
    in_specs = (P("row", "col", None, None), P(), P())
    out_specs = (P("row", "col", None, None), P("row", "col", None, None))
    return jax.shard_map(
        on_device, mesh=mesh, in_specs=in_specs, out_specs=out_specs, check_vma=False
    )
```

```python
import functools
import math

import jax
import jax.numpy as jnp
from jax import lax
from jax.experimental import pallas as pl
from jax.experimental.pallas import tpu as pltpu
from jax.sharding import PartitionSpec as P

NZ = 12
MESH = pl.DeviceIdType.MESH


def halves(x):
    high = x.astype(jnp.bfloat16)
    low = (x - high.astype(jnp.float32)).astype(jnp.bfloat16)
    return high, low


def kernel(
    row_count, chips, chunks,
    place_ref, pattern_ref, blocks_ref,
    square_ref, update_ref,
    left, right, square_panel, square_high, square_low, outgoing, incoming,
    index_ref, order_ref, square_row_ref, update_row_ref,
    left_send, left_recv, right_send, right_recv, panel_send, panel_recv, update_send, update_recv,
):
    group_rows, slots, edge = blocks_ref.shape[0], blocks_ref.shape[1], blocks_ref.shape[2]
    columns = 2 * chips
    capacity = group_rows // row_count
    height = group_rows // chunks
    all_slots = columns * slots
    grid_mesh = row_count == 4
    r = lax.axis_index("row")
    c = lax.axis_index("col")
    z = c // 2
    core = c % 2
    sibling = z * 2 + 1 - core
    x_side = r + 1 - 2 * (r % 2)
    y_side = lax.rem(r + 2, 4)
    start_scale = 1.0 / math.sqrt(NZ * edge)

    barrier = pltpu.get_barrier_semaphore()

    def greet(row, col):
        pl.semaphore_signal(barrier, inc=1, device_id=(row, col), device_id_type=MESH)

    greet(r, sibling)
    for d in range(1, row_count):
        greet(lax.rem(r + d, row_count), c)

    @pl.when(z > 0)
    def _():
        greet(r, c - 2)

    @pl.when(z < chips - 1)
    def _():
        greet(r, c + 2)

    zero_block = group_rows * row_count * slots
    right[zero_block] = jnp.zeros((edge, edge), jnp.float32)
    square_high[zero_block] = jnp.zeros((edge, edge), jnp.bfloat16)
    square_low[zero_block] = jnp.zeros((edge, edge), jnp.bfloat16)

    def bring(q, carry):
        row = blocks_ref[q]
        left[c, q] = row
        for s in range(slots):
            right[(r * group_rows + q) * slots + s] = row[s]
        return carry

    lax.fori_loop(0, group_rows, bring, 0)

    has_lower = (z + chips - 1) // chips
    has_upper = 1 - z // (chips - 1)
    pl.semaphore_wait(barrier, row_count + has_lower + has_upper)
    middle = has_lower * has_upper
    lead = 2 * middle
    ahead = 4 - 2 * middle

    def part_copy(panel, send, recv, size, source, part, way, target):
        span = panel.at[pl.ds(source * group_rows * slots + part * size, size)]
        return pltpu.make_async_remote_copy(
            src_ref=span, dst_ref=span, send_sem=send.at[way, part], recv_sem=recv.at[source, part],
            device_id=(target, c), device_id_type=MESH,
        )

    def part_wait(panel, send, recv, size, source, part):
        part_copy(panel, send, recv, size, source, part, 0, lax.rem(r + 1, row_count)).wait_recv()

    def spread(panel, send, recv, size, first, turn):
        if grid_mesh:
            for part, way in ((0, 0), (1, 1)) if turn == 0 else ((1, 0), (0, 1)):
                target = x_side if way == 0 else y_side
                part_copy(panel, send, recv, size, r, first + part, way, target).start()
        else:
            for d in range(1, row_count):
                part_copy(panel, send, recv, size, r, first + turn, d - 1, lax.rem(r + d, row_count)).start()

    def pass_on(panel, send, recv, size, first):
        if grid_mesh:
            part_wait(panel, send, recv, size, x_side, first)
            part_copy(panel, send, recv, size, x_side, first, 2, y_side).start()
            part_wait(panel, send, recv, size, y_side, first + 1)
            part_copy(panel, send, recv, size, y_side, first + 1, 3, x_side).start()

    def gather_rest(panel, send, recv, size, first):
        if grid_mesh:
            part_wait(panel, send, recv, size, x_side, first + 1)
            part_wait(panel, send, recv, size, y_side, first)
            part_wait(panel, send, recv, size, 3 - r, first)
            part_wait(panel, send, recv, size, 3 - r, first + 1)
        else:
            for part in (0, 1):
                for d in range(1, row_count):
                    part_wait(panel, send, recv, size, lax.rem(r + d, row_count), first + part)

    def sent(panel, send, recv, size, first):
        if grid_mesh:
            ways = ((0, 0), (1, 0), (0, 1), (1, 1), (0, 2), (1, 3))
        else:
            ways = [(part, d) for part in (0, 1) for d in range(row_count - 1)]
        for part, way in ways:
            part_copy(panel, send, recv, size, r, first + part, way, lax.rem(r + 1, row_count)).wait_send()

    matrix_side = (right, right_send, right_recv, group_rows * slots // 2)
    square_side = (square_panel, panel_send, panel_recv, height * slots // 2)

    def left_copy(source, chunk, way, target):
        span = left.at[source, pl.ds(chunk * height, height)]
        return pltpu.make_async_remote_copy(
            src_ref=span, dst_ref=span, send_sem=left_send.at[way, source, chunk],
            recv_sem=left_recv.at[source, chunk], device_id=(r, target), device_id_type=MESH,
        )

    def own_left(chunk):
        @pl.when(z < chips - 1)
        def _():
            left_copy(c, chunk, 0, c + 2).start()

        @pl.when(z > 0)
        def _():
            left_copy(c, chunk, 1, c - 2).start()

        left_copy(c, chunk, 2, sibling).start()

    def advance(chunk):
        @pl.when(chunk + ahead < chunks)
        def _():
            own_left(chunk + ahead)

        for d in range(1, chips):
            @pl.when(z - d >= 0)
            def _():
                source = c - 2 * d
                left_copy(source, chunk, 0, sibling).wait_recv()

                @pl.when(z < chips - 1)
                def _():
                    left_copy(source, chunk, 0, c + 2).start()

                left_copy(source, chunk, 2, sibling).start()

            @pl.when(z + d < chips)
            def _():
                source = c + 2 * d
                left_copy(source, chunk, 0, sibling).wait_recv()

                @pl.when(z > 0)
                def _():
                    left_copy(source, chunk, 1, c - 2).start()

                left_copy(source, chunk, 2, sibling).start()

    def left_rest(chunk):
        def one(p, carry):
            left_copy(2 * p + 1 - core, chunk, 0, sibling).wait_recv()
            return carry

        lax.fori_loop(0, chips, one, 0)

    def left_sent(chunk, carry):
        def one(p, carry):
            source = 2 * p + core

            @pl.when((p <= z) & (z < chips - 1))
            def _():
                left_copy(source, chunk, 0, sibling).wait_send()

            @pl.when((p >= z) & (z > 0))
            def _():
                left_copy(source, chunk, 1, sibling).wait_send()

            left_copy(source, chunk, 2, sibling).wait_send()
            return carry

        lax.fori_loop(0, chips, one, 0)
        return carry

    def make_index(q, carry):
        atom = r * group_rows + q
        wanted = [pattern_ref[atom, c * slots + t] for t in range(slots)]
        for u in range(all_slots):
            neighbour = pattern_ref[atom, u]
            at = jnp.maximum(neighbour, 0)
            held = [pattern_ref[at, c * slots + v] for v in range(slots)]
            for t in range(slots):
                place = zero_block
                for v in range(slots):
                    place = jnp.where(held[v] == wanted[t], at * slots + v, place)
                place = jnp.where((neighbour >= 0) & (wanted[t] >= 0), place, zero_block)
                index_ref[(q * all_slots + u) * slots + t] = place
        return carry

    def make_order(place, carry):
        target, number = place // capacity, place % capacity
        found, count = jnp.int32(0), jnp.int32(0)
        for i in range(group_rows):
            hit = (place_ref[r * group_rows + i] // group_rows == target).astype(jnp.int32)
            found = jnp.where((hit == 1) & (count == number), i, found)
            count = count + hit
        order_ref[place] = found
        return carry

    def make_rows(p, carry):
        def look(a, found):
            return jnp.where(place_ref[a] == r * group_rows + p, a, found)

        atom = lax.fori_loop(0, row_count * group_rows, look, jnp.int32(0), unroll=8)
        source = atom // group_rows
        count = jnp.int32(0)
        for i in range(group_rows):
            hit = (place_ref[source * group_rows + i] // group_rows == r) & (i < atom % group_rows)
            count = count + hit.astype(jnp.int32)
        square_row_ref[p] = atom
        update_row_ref[p] = source * capacity + jnp.minimum(count, capacity - 1)
        return carry

    def product(q, panels):
        total = jnp.zeros((edge, slots * edge), jnp.float32)
        for p in range(columns):
            row = left[p, q]
            a_high, a_low = halves(jnp.concatenate([row[u] for u in range(slots)], axis=1))

            def weights(panel):
                return jnp.concatenate(
                    [
                        jnp.concatenate(
                            [panel[index_ref[(q * all_slots + p * slots + u) * slots + t]] for t in range(slots)],
                            axis=1,
                        )
                        for u in range(slots)
                    ],
                    axis=0,
                )

            if len(panels) == 1:
                b_high, b_low = halves(weights(panels[0]))
            else:
                b_high, b_low = weights(panels[0]), weights(panels[1])
            both = jnp.concatenate([a_high, a_low], axis=0)
            by_high = jnp.dot(both, b_high, preferred_element_type=jnp.float32)
            by_low = jnp.dot(a_high, b_low, preferred_element_type=jnp.float32)
            total = total + (by_high[:edge] + (by_high[edge:] + by_low))
        return total

    def square_chunk(chunk):
        left_rest(chunk)

        def one(k, carry):
            q = chunk * height + k
            total = product(q, (right,)) * start_scale
            for t in range(slots):
                square_panel[(r * group_rows + q) * slots + t] = total[:, t * edge : (t + 1) * edge]
            return carry

        lax.fori_loop(0, height, one, 0)
        spread(*square_side, 2 * chunk, 0)
        spread(*square_side, 2 * chunk, 1)

    def finish_chunk(chunk):
        gather_rest(*square_side, 2 * chunk)

        def one(source, carry):
            first = (source * group_rows + chunk * height) * slots
            for b in range(height * slots):
                high, low = halves(square_panel[first + b])
                square_high[first + b] = high
                square_low[first + b] = low
            return carry

        lax.fori_loop(0, row_count, one, 0)

    def advance_from(first, last):
        lax.fori_loop(first, last, lambda h, carry: (advance(h), carry)[1], 0)

    half = chunks // 2
    quarter = half // 2
    spread(*matrix_side, 0, 0)
    lax.fori_loop(0, ahead, lambda h, carry: (own_left(h), carry)[1], 0)
    lax.fori_loop(0, group_rows, make_index, 0)
    advance_from(0, half // 4)
    spread(*matrix_side, 0, 1)
    lax.fori_loop(0, group_rows, make_order, 0)
    lax.fori_loop(0, group_rows, make_rows, 0)
    advance_from(half // 4, half // 2)
    pass_on(*matrix_side, 0)
    advance_from(half // 2, half + lead)
    gather_rest(*matrix_side, 0)

    lax.fori_loop(0, quarter, lambda m, carry: (square_chunk(m), carry)[1], 0)

    def advance_late(chunk):
        @pl.when(chunk < chunks)
        def _():
            advance(chunk)

    def second(k, carry):
        advance_late(half + lead + k)
        pass_on(*square_side, 4 * k)
        pass_on(*square_side, 4 * k + 2)
        square_chunk(quarter + 2 * k)
        square_chunk(quarter + 2 * k + 1)

        @pl.when(k > 0)
        def _():
            finish_chunk(2 * k - 2)
            finish_chunk(2 * k - 1)

        return carry

    def third(k, carry):
        advance_late(half + quarter + lead + k)
        square_chunk(half + quarter + k)

        @pl.when(k < quarter // 2)
        def _():
            pass_on(*square_side, 2 * (half + 2 * k))
            pass_on(*square_side, 2 * (half + 2 * k + 1))

        @pl.when(k >= quarter // 2)
        def _():
            pass_on(*square_side, 2 * (half + quarter // 2 + k))

        @pl.when(k <= quarter // 2)
        def _():
            finish_chunk(half - 2 + 2 * k)
            finish_chunk(half - 1 + 2 * k)

        return carry

    lax.fori_loop(0, quarter, second, 0)
    lax.fori_loop(0, quarter, third, 0)
    lax.fori_loop(
        half + quarter + quarter // 2, chunks, lambda m, carry: (pass_on(*square_side, 2 * m), carry)[1], 0
    )
    lax.fori_loop(half + quarter, chunks, lambda m, carry: (finish_chunk(m), carry)[1], 0)

    def update_rows(target, store):
        def one(k, carry):
            q = order_ref[target * capacity + k]
            total = product(q, (square_high, square_low)) * (0.5 * start_scale)
            for t in range(slots):
                filled = pattern_ref[r * group_rows + q, c * slots + t] >= 0
                own = left[c, q, t] * jnp.where(filled, 1.5, 0.0)
                store(k, t, own - total[:, t * edge : (t + 1) * edge])
            return carry

        lax.fori_loop(0, capacity, one, 0)

    ways = [row_count - 1] + list(range(1, row_count - 1)) if not grid_mesh else [3, 1, 2]
    def target_of(way):
        if not grid_mesh:
            return lax.rem(r + way, row_count)
        return {1: x_side, 2: y_side, 3: 3 - r}[way]

    for way in ways:
        target = target_of(way)

        def store(k, t, value):
            outgoing[target * capacity + k, t] = value

        update_rows(target, store)
        pltpu.make_async_remote_copy(
            src_ref=outgoing.at[pl.ds(target * capacity, capacity)],
            dst_ref=incoming.at[pl.ds(r * capacity, capacity)],
            send_sem=update_send.at[way], recv_sem=update_recv.at[r],
            device_id=(target, c), device_id_type=MESH,
        ).start()

    def keep(k, t, value):
        incoming[r * capacity + k, t] = value

    update_rows(r, keep)

    def square_out(p, carry):
        row = square_row_ref[p]
        for t in range(slots):
            square_ref[p, t] = square_panel[row * slots + t]
        return carry

    lax.fori_loop(0, group_rows, square_out, 0)

    for way in ways:
        source = target_of(way) if grid_mesh else lax.rem(r + row_count - way, row_count)
        pltpu.make_async_remote_copy(
            src_ref=outgoing.at[pl.ds(0, capacity)],
            dst_ref=incoming.at[pl.ds(source * capacity, capacity)],
            send_sem=update_send.at[way], recv_sem=update_recv.at[source],
            device_id=(lax.rem(r + 1, row_count), c), device_id_type=MESH,
        ).wait()

    def update_out(p, carry):
        update_ref[p] = incoming[update_row_ref[p]]
        return carry

    lax.fori_loop(0, group_rows, update_out, 0)

    sent(*matrix_side, 0)

    def all_sent(chunk, carry):
        sent(*square_side, 2 * chunk)
        return carry

    lax.fori_loop(0, chunks, all_sent, 0)
    lax.fori_loop(0, chunks, left_sent, 0)


def on_device(atom_blocks, grid_position, pattern):
    group_rows, slots, edge = atom_blocks.shape[:3]
    row_count, columns = lax.axis_size("row"), lax.axis_size("col")
    chips = columns // 2
    chunks = group_rows * slots // 2
    panel = (group_rows * row_count * slots + 1, edge, edge)
    ways = max(row_count, 4)
    smem = pl.BlockSpec(memory_space=pltpu.SMEM)
    vmem = pl.BlockSpec(memory_space=pltpu.VMEM)
    dma = pltpu.SemaphoreType.DMA
    out = jax.ShapeDtypeStruct(atom_blocks.shape, jnp.float32)
    return pl.pallas_call(
        functools.partial(kernel, row_count, chips, chunks),
        out_shape=(out, out),
        in_specs=[smem] * 2 + [vmem],
        out_specs=(vmem, vmem),
        scratch_shapes=[
            pltpu.VMEM((columns, group_rows, slots, edge, edge), jnp.float32),
            pltpu.VMEM(panel, jnp.float32),
            pltpu.VMEM(panel, jnp.float32),
            pltpu.VMEM(panel, jnp.bfloat16),
            pltpu.VMEM(panel, jnp.bfloat16),
            pltpu.VMEM((group_rows, slots, edge, edge), jnp.float32),
            pltpu.VMEM((group_rows, slots, edge, edge), jnp.float32),
            pltpu.SMEM((group_rows * columns * slots * slots,), jnp.int32),
            pltpu.SMEM((group_rows,), jnp.int32),
            pltpu.SMEM((group_rows,), jnp.int32),
            pltpu.SMEM((group_rows,), jnp.int32),
            dma((3, columns, chunks)),
            dma((columns, chunks)),
            dma((ways, 2)),
            dma((row_count, 2)),
            dma((ways, 2 * chunks)),
            dma((row_count, 2 * chunks)),
            dma((ways,)),
            dma((row_count,)),
        ],
        compiler_params=pltpu.CompilerParams(
            collective_id=0, has_side_effects=True, vmem_limit_bytes=56 * 2**20
        ),
        cost_estimate=pl.CostEstimate(
            flops=12 * group_rows * columns * slots * slots * edge**3,
            bytes_accessed=12 * group_rows * slots * edge * edge,
            transcendentals=0,
        ),
    )(grid_position, pattern, atom_blocks)


def solution(mesh):
    in_specs = (P("row", "col", None, None), P(), P())
    out_specs = (P("row", "col", None, None), P("row", "col", None, None))
    return jax.shard_map(
        on_device, mesh=mesh, in_specs=in_specs, out_specs=out_specs, check_vma=False
    )
```

```python
import functools
import math

import jax
import jax.numpy as jnp
from jax import lax
from jax.experimental import pallas as pl
from jax.experimental.pallas import tpu as pltpu
from jax.sharding import PartitionSpec as P

NZ = 12
MESH = pl.DeviceIdType.MESH


def halves(x):
    high = x.astype(jnp.bfloat16)
    low = (x - high.astype(jnp.float32)).astype(jnp.bfloat16)
    return high, low


def kernel(
    row_count, chips, chunks,
    place_ref, pattern_ref, blocks_ref,
    square_ref, update_ref,
    left, right, square_panel, square_high, square_low, outgoing, incoming,
    index_ref, order_ref, square_row_ref, update_row_ref,
    left_send, left_recv, right_send, right_recv, panel_send, panel_recv, update_send, update_recv,
):
    group_rows, slots, edge = blocks_ref.shape[0], blocks_ref.shape[1], blocks_ref.shape[2]
    columns = 2 * chips
    capacity = group_rows // row_count
    height = group_rows // chunks
    all_slots = columns * slots
    grid_mesh = row_count == 4
    r = lax.axis_index("row")
    c = lax.axis_index("col")
    z = c // 2
    core = c % 2
    sibling = z * 2 + 1 - core
    x_side = r + 1 - 2 * (r % 2)
    y_side = lax.rem(r + 2, 4)
    start_scale = 1.0 / math.sqrt(NZ * edge)

    barrier = pltpu.get_barrier_semaphore()

    def greet(row, col):
        pl.semaphore_signal(barrier, inc=1, device_id=(row, col), device_id_type=MESH)

    greet(r, sibling)
    for d in range(1, row_count):
        greet(lax.rem(r + d, row_count), c)

    @pl.when(z > 0)
    def _():
        greet(r, c - 2)

    @pl.when(z < chips - 1)
    def _():
        greet(r, c + 2)

    zero_block = group_rows * row_count * slots
    right[zero_block] = jnp.zeros((edge, edge), jnp.float32)
    square_high[zero_block] = jnp.zeros((edge, edge), jnp.bfloat16)
    square_low[zero_block] = jnp.zeros((edge, edge), jnp.bfloat16)

    def bring(q, carry):
        row = blocks_ref[q]
        left[c, q] = row
        for s in range(slots):
            right[(r * group_rows + q) * slots + s] = row[s]
        return carry

    lax.fori_loop(0, group_rows, bring, 0)

    has_lower = (z + chips - 1) // chips
    has_upper = 1 - z // (chips - 1)
    pl.semaphore_wait(barrier, row_count + has_lower + has_upper)
    middle = has_lower * has_upper
    lead = 3 * middle
    ahead = 5 - 2 * middle

    def part_copy(panel, send, recv, size, source, part, way, target):
        span = panel.at[pl.ds(source * group_rows * slots + part * size, size)]
        return pltpu.make_async_remote_copy(
            src_ref=span, dst_ref=span, send_sem=send.at[way, part], recv_sem=recv.at[source, part],
            device_id=(target, c), device_id_type=MESH,
        )

    def part_wait(panel, send, recv, size, source, part):
        part_copy(panel, send, recv, size, source, part, 0, lax.rem(r + 1, row_count)).wait_recv()

    def spread(panel, send, recv, size, first, turn):
        if grid_mesh:
            for part, way in ((0, 0), (1, 1)) if turn == 0 else ((1, 0), (0, 1)):
                target = x_side if way == 0 else y_side
                part_copy(panel, send, recv, size, r, first + part, way, target).start()
        else:
            for d in range(1, row_count):
                part_copy(panel, send, recv, size, r, first + turn, d - 1, lax.rem(r + d, row_count)).start()

    def pass_on(panel, send, recv, size, first):
        if grid_mesh:
            part_wait(panel, send, recv, size, x_side, first)
            part_copy(panel, send, recv, size, x_side, first, 2, y_side).start()
            part_wait(panel, send, recv, size, y_side, first + 1)
            part_copy(panel, send, recv, size, y_side, first + 1, 3, x_side).start()

    def gather_rest(panel, send, recv, size, first):
        if grid_mesh:
            part_wait(panel, send, recv, size, x_side, first + 1)
            part_wait(panel, send, recv, size, y_side, first)
            part_wait(panel, send, recv, size, 3 - r, first)
            part_wait(panel, send, recv, size, 3 - r, first + 1)
        else:
            for part in (0, 1):
                for d in range(1, row_count):
                    part_wait(panel, send, recv, size, lax.rem(r + d, row_count), first + part)

    def sent(panel, send, recv, size, first):
        if grid_mesh:
            ways = ((0, 0), (1, 0), (0, 1), (1, 1), (0, 2), (1, 3))
        else:
            ways = [(part, d) for part in (0, 1) for d in range(row_count - 1)]
        for part, way in ways:
            part_copy(panel, send, recv, size, r, first + part, way, lax.rem(r + 1, row_count)).wait_send()

    matrix_side = (right, right_send, right_recv, group_rows * slots // 2)
    square_side = (square_panel, panel_send, panel_recv, height * slots // 2)

    def left_copy(source, chunk, way, target):
        span = left.at[source, pl.ds(chunk * height, height)]
        return pltpu.make_async_remote_copy(
            src_ref=span, dst_ref=span, send_sem=left_send.at[way, source, chunk],
            recv_sem=left_recv.at[source, chunk], device_id=(r, target), device_id_type=MESH,
        )

    def own_left(chunk):
        @pl.when(z < chips - 1)
        def _():
            left_copy(c, chunk, 0, c + 2).start()

        @pl.when(z > 0)
        def _():
            left_copy(c, chunk, 1, c - 2).start()

        left_copy(c, chunk, 2, sibling).start()

    def advance(chunk):
        @pl.when(chunk + ahead < chunks)
        def _():
            own_left(chunk + ahead)

        for d in range(1, chips):
            @pl.when(z - d >= 0)
            def _():
                source = c - 2 * d
                left_copy(source, chunk, 0, sibling).wait_recv()

                @pl.when(z < chips - 1)
                def _():
                    left_copy(source, chunk, 0, c + 2).start()

                left_copy(source, chunk, 2, sibling).start()

            @pl.when(z + d < chips)
            def _():
                source = c + 2 * d
                left_copy(source, chunk, 0, sibling).wait_recv()

                @pl.when(z > 0)
                def _():
                    left_copy(source, chunk, 1, c - 2).start()

                left_copy(source, chunk, 2, sibling).start()

    def left_rest(chunk):
        def one(p, carry):
            left_copy(2 * p + 1 - core, chunk, 0, sibling).wait_recv()
            return carry

        lax.fori_loop(0, chips, one, 0)

    def left_sent(chunk, carry):
        def one(p, carry):
            source = 2 * p + core

            @pl.when((p <= z) & (z < chips - 1))
            def _():
                left_copy(source, chunk, 0, sibling).wait_send()

            @pl.when((p >= z) & (z > 0))
            def _():
                left_copy(source, chunk, 1, sibling).wait_send()

            left_copy(source, chunk, 2, sibling).wait_send()
            return carry

        lax.fori_loop(0, chips, one, 0)
        return carry

    def make_index(q, carry):
        atom = r * group_rows + q
        wanted = [pattern_ref[atom, c * slots + t] for t in range(slots)]
        for u in range(all_slots):
            neighbour = pattern_ref[atom, u]
            at = jnp.maximum(neighbour, 0)
            held = [pattern_ref[at, c * slots + v] for v in range(slots)]
            for t in range(slots):
                place = zero_block
                for v in range(slots):
                    place = jnp.where(held[v] == wanted[t], at * slots + v, place)
                place = jnp.where((neighbour >= 0) & (wanted[t] >= 0), place, zero_block)
                index_ref[(q * all_slots + u) * slots + t] = place
        return carry

    def make_order(place, carry):
        target, number = place // capacity, place % capacity
        found, count = jnp.int32(0), jnp.int32(0)
        for i in range(group_rows):
            hit = (place_ref[r * group_rows + i] // group_rows == target).astype(jnp.int32)
            found = jnp.where((hit == 1) & (count == number), i, found)
            count = count + hit
        order_ref[place] = found
        return carry

    def make_rows(p, carry):
        def look(a, found):
            return jnp.where(place_ref[a] == r * group_rows + p, a, found)

        atom = lax.fori_loop(0, row_count * group_rows, look, jnp.int32(0), unroll=8)
        source = atom // group_rows
        count = jnp.int32(0)
        for i in range(group_rows):
            hit = (place_ref[source * group_rows + i] // group_rows == r) & (i < atom % group_rows)
            count = count + hit.astype(jnp.int32)
        square_row_ref[p] = atom
        update_row_ref[p] = source * capacity + jnp.minimum(count, capacity - 1)
        return carry

    def product(q, panels):
        total = jnp.zeros((edge, slots * edge), jnp.float32)
        for p in range(columns):
            row = left[p, q]
            a_high, a_low = halves(jnp.concatenate([row[u] for u in range(slots)], axis=1))

            def weights(panel):
                return jnp.concatenate(
                    [
                        jnp.concatenate(
                            [panel[index_ref[(q * all_slots + p * slots + u) * slots + t]] for t in range(slots)],
                            axis=1,
                        )
                        for u in range(slots)
                    ],
                    axis=0,
                )

            if len(panels) == 1:
                b_high, b_low = halves(weights(panels[0]))
            else:
                b_high, b_low = weights(panels[0]), weights(panels[1])
            both = jnp.concatenate([a_high, a_low], axis=0)
            by_high = jnp.dot(both, b_high, preferred_element_type=jnp.float32)
            by_low = jnp.dot(a_high, b_low, preferred_element_type=jnp.float32)
            total = total + (by_high[:edge] + (by_high[edge:] + by_low))
        return total

    def square_chunk(chunk):
        left_rest(chunk)

        def one(k, carry):
            q = chunk * height + k
            total = product(q, (right,)) * start_scale
            for t in range(slots):
                square_panel[(r * group_rows + q) * slots + t] = total[:, t * edge : (t + 1) * edge]
            return carry

        lax.fori_loop(0, height, one, 0)
        spread(*square_side, 2 * chunk, 0)
        spread(*square_side, 2 * chunk, 1)

    def finish_chunk(chunk):
        gather_rest(*square_side, 2 * chunk)

        def one(source, carry):
            first = (source * group_rows + chunk * height) * slots
            for b in range(height * slots):
                high, low = halves(square_panel[first + b])
                square_high[first + b] = high
                square_low[first + b] = low
            return carry

        lax.fori_loop(0, row_count, one, 0)

    def advance_from(first, last):
        lax.fori_loop(first, last, lambda h, carry: (advance(h), carry)[1], 0)

    half = chunks // 2
    quarter = half // 2
    lax.fori_loop(0, ahead, lambda h, carry: (own_left(h), carry)[1], 0)
    spread(*matrix_side, 0, 0)
    lax.fori_loop(0, group_rows, make_index, 0)
    advance_from(0, half // 4)
    spread(*matrix_side, 0, 1)
    lax.fori_loop(0, group_rows, make_order, 0)
    lax.fori_loop(0, group_rows, make_rows, 0)
    advance_from(half // 4, half // 2)
    pass_on(*matrix_side, 0)
    advance_from(half // 2, half + lead)
    gather_rest(*matrix_side, 0)

    lax.fori_loop(0, quarter, lambda m, carry: (square_chunk(m), carry)[1], 0)

    def advance_late(chunk):
        @pl.when(chunk < chunks)
        def _():
            advance(chunk)

    def second(k, carry):
        advance_late(half + lead + k)
        pass_on(*square_side, 4 * k)
        pass_on(*square_side, 4 * k + 2)
        square_chunk(quarter + 2 * k)
        square_chunk(quarter + 2 * k + 1)

        @pl.when(k > 0)
        def _():
            finish_chunk(2 * k - 2)
            finish_chunk(2 * k - 1)

        return carry

    def third(k, carry):
        advance_late(half + quarter + lead + k)
        square_chunk(half + quarter + k)

        @pl.when(k < quarter // 2)
        def _():
            pass_on(*square_side, 2 * (half + 2 * k))
            pass_on(*square_side, 2 * (half + 2 * k + 1))

        @pl.when(k >= quarter // 2)
        def _():
            pass_on(*square_side, 2 * (half + quarter // 2 + k))

        @pl.when(k <= quarter // 2)
        def _():
            finish_chunk(half - 2 + 2 * k)
            finish_chunk(half - 1 + 2 * k)

        return carry

    lax.fori_loop(0, quarter, second, 0)
    lax.fori_loop(0, quarter, third, 0)
    lax.fori_loop(
        half + quarter + quarter // 2, chunks, lambda m, carry: (pass_on(*square_side, 2 * m), carry)[1], 0
    )
    lax.fori_loop(half + quarter, chunks, lambda m, carry: (finish_chunk(m), carry)[1], 0)

    def update_rows(target, store):
        def one(k, carry):
            q = order_ref[target * capacity + k]
            total = product(q, (square_high, square_low)) * (0.5 * start_scale)
            for t in range(slots):
                filled = pattern_ref[r * group_rows + q, c * slots + t] >= 0
                own = left[c, q, t] * jnp.where(filled, 1.5, 0.0)
                store(k, t, own - total[:, t * edge : (t + 1) * edge])
            return carry

        lax.fori_loop(0, capacity, one, 0)

    ways = [row_count - 1] + list(range(1, row_count - 1)) if not grid_mesh else [3, 1, 2]
    def target_of(way):
        if not grid_mesh:
            return lax.rem(r + way, row_count)
        return {1: x_side, 2: y_side, 3: 3 - r}[way]

    for way in ways:
        target = target_of(way)

        def store(k, t, value):
            outgoing[target * capacity + k, t] = value

        update_rows(target, store)
        pltpu.make_async_remote_copy(
            src_ref=outgoing.at[pl.ds(target * capacity, capacity)],
            dst_ref=incoming.at[pl.ds(r * capacity, capacity)],
            send_sem=update_send.at[way], recv_sem=update_recv.at[r],
            device_id=(target, c), device_id_type=MESH,
        ).start()

    def keep(k, t, value):
        incoming[r * capacity + k, t] = value

    update_rows(r, keep)

    def square_out(p, carry):
        row = square_row_ref[p]
        for t in range(slots):
            square_ref[p, t] = square_panel[row * slots + t]
        return carry

    lax.fori_loop(0, group_rows, square_out, 0)

    for way in ways:
        source = target_of(way) if grid_mesh else lax.rem(r + row_count - way, row_count)
        pltpu.make_async_remote_copy(
            src_ref=outgoing.at[pl.ds(0, capacity)],
            dst_ref=incoming.at[pl.ds(source * capacity, capacity)],
            send_sem=update_send.at[way], recv_sem=update_recv.at[source],
            device_id=(lax.rem(r + 1, row_count), c), device_id_type=MESH,
        ).wait()

    def update_out(p, carry):
        update_ref[p] = incoming[update_row_ref[p]]
        return carry

    lax.fori_loop(0, group_rows, update_out, 0)

    sent(*matrix_side, 0)

    def all_sent(chunk, carry):
        sent(*square_side, 2 * chunk)
        return carry

    lax.fori_loop(0, chunks, all_sent, 0)
    lax.fori_loop(0, chunks, left_sent, 0)


def on_device(atom_blocks, grid_position, pattern):
    group_rows, slots, edge = atom_blocks.shape[:3]
    row_count, columns = lax.axis_size("row"), lax.axis_size("col")
    chips = columns // 2
    chunks = group_rows * slots // 2
    panel = (group_rows * row_count * slots + 1, edge, edge)
    ways = max(row_count, 4)
    smem = pl.BlockSpec(memory_space=pltpu.SMEM)
    vmem = pl.BlockSpec(memory_space=pltpu.VMEM)
    dma = pltpu.SemaphoreType.DMA
    out = jax.ShapeDtypeStruct(atom_blocks.shape, jnp.float32)
    return pl.pallas_call(
        functools.partial(kernel, row_count, chips, chunks),
        out_shape=(out, out),
        in_specs=[smem] * 2 + [vmem],
        out_specs=(vmem, vmem),
        scratch_shapes=[
            pltpu.VMEM((columns, group_rows, slots, edge, edge), jnp.float32),
            pltpu.VMEM(panel, jnp.float32),
            pltpu.VMEM(panel, jnp.float32),
            pltpu.VMEM(panel, jnp.bfloat16),
            pltpu.VMEM(panel, jnp.bfloat16),
            pltpu.VMEM((group_rows, slots, edge, edge), jnp.float32),
            pltpu.VMEM((group_rows, slots, edge, edge), jnp.float32),
            pltpu.SMEM((group_rows * columns * slots * slots,), jnp.int32),
            pltpu.SMEM((group_rows,), jnp.int32),
            pltpu.SMEM((group_rows,), jnp.int32),
            pltpu.SMEM((group_rows,), jnp.int32),
            dma((3, columns, chunks)),
            dma((columns, chunks)),
            dma((ways, 2)),
            dma((row_count, 2)),
            dma((ways, 2 * chunks)),
            dma((row_count, 2 * chunks)),
            dma((ways,)),
            dma((row_count,)),
        ],
        compiler_params=pltpu.CompilerParams(
            collective_id=0, has_side_effects=True, vmem_limit_bytes=56 * 2**20
        ),
        cost_estimate=pl.CostEstimate(
            flops=12 * group_rows * columns * slots * slots * edge**3,
            bytes_accessed=12 * group_rows * slots * edge * edge,
            transcendentals=0,
        ),
    )(grid_position, pattern, atom_blocks)


def solution(mesh):
    in_specs = (P("row", "col", None, None), P(), P())
    out_specs = (P("row", "col", None, None), P("row", "col", None, None))
    return jax.shard_map(
        on_device, mesh=mesh, in_specs=in_specs, out_specs=out_specs, check_vma=False
    )
```
